128 devices in a mesh: img: 8 (over z, y_hi), ref: 16 (over x, y_lo, core).
Axes of the slice: x: 4, y: 4 (y_hi: 2, y_lo: 2; y = y_hi * 2 + y_lo), z: 4, core: 2. Of those that a mesh axis runs over, the one named last changes fastest.
Arguments:
- images: bfloat16 [8192, 9216], P(('img', 'ref')), may hold values from -96 to 96
- references: bfloat16 [6912, 9216], P('ref'), may hold values from -0.5 to 0.5
- class_prior: float32 [192], P('ref'), may hold values from 0.2 to 5
Outputs:
- class_sums: float32 [192, 9216], P('ref', 'img')
- class_weights: float32 [192], P('ref')
The draws below stay inside these ranges and needn't reach their ends.
All inputs are finite; a program needn't handle non-finite values.
Results may differ from the reference program's by a relative error of at most 0.0021.
Values may be sent and summed in bfloat16 or wider, within the bound.
A program may use at most 128 MiB of HBM per device.

```python
import math
import jax
import jax.numpy as jnp
from jax import lax

RAD = 64
ANG = 144
ROT = 36
K = 192
IMG_DEV = 64
NIMG = 8192
N_REF = 16


def class_library(key):
    inner = jax.random.fold_in(key, 11)
    first_key, second_key = jax.random.split(inner)
    ranks = jnp.arange(K).astype(jnp.float32)
    scales = 3.0 ** (ranks / (K - 1)) * jnp.exp(jax.random.uniform(first_key, (K,), jnp.float32, jnp.log(0.5), 0.0))
    templates = jax.random.normal(second_key, (K, RAD, ANG), jnp.float32) * scales[:, None, None] / jnp.sqrt(1.0 * RAD * ANG)
    return templates


def draw_references(key, part):
    templates = class_library(key)
    turned = jnp.stack([jnp.roll(templates, turn_index * (ANG // ROT), axis=2) for turn_index in range(ROT)], axis=1)
    return turned.reshape(K * ROT, RAD * ANG).astype(jnp.bfloat16)


def draw_images(key, part):
    inner = jax.random.fold_in(key, 21)
    keys = jax.random.split(inner, 2)
    rows = jnp.arange(NIMG).astype(jnp.float32)
    rising = 1.0 + 2.0 * rows / (NIMG - 1)
    jitter = jnp.exp(jax.random.uniform(keys[0], (NIMG,), jnp.float32, jnp.log(0.7), jnp.log(1.4)))
    noise = jax.random.normal(keys[1], (NIMG, RAD * ANG), jnp.float32)
    images = noise * (rising * jitter)[:, None]
    return images.astype(jnp.bfloat16)


def level_of(stream_key, shape, cuts, low, largest):
    def one(dim, blocks):
        draws = jax.random.uniform(jax.random.fold_in(jax.random.fold_in(stream_key, 6), dim), (blocks,), jnp.float32, low / len(cuts), largest / len(cuts))
        return jnp.repeat(jnp.exp(draws), shape[dim] // blocks).reshape((-1,) + (1,) * (len(shape) - dim - 1))

    level = one(*cuts[0])
    for cut in cuts[1:]:
        level = level * one(*cut)
    return level


def setup_inputs(seed: int = 0) -> dict:
    key_of = jax.random.split(jax.random.key(seed), 4)
    return {
        "images": draw_images(jax.random.fold_in(key_of[3], 71), 0),
        "references": draw_references(jax.random.fold_in(key_of[3], 71), 0),
        "class_prior": jnp.clip(jnp.exp(math.log(5.0) - 3.218876 * jax.random.uniform(key_of[2], (K,), jnp.float32) ** level_of(key_of[2], (K,), ((0, 16),), -0.2, 0.2)), 0.2, 5.0),
    }


def reference(images, references, class_prior):
    shift_size = ANG // ROT
    grouped = references.reshape(K, ROT, RAD * ANG)
    half_norm = lax.map(lambda block: 0.5 * jnp.sum(jnp.square(block.astype(jnp.float32)), axis=-1), grouped).reshape(K * ROT)
    offsets = jnp.repeat(jnp.log(class_prior), ROT) - half_norm
    group_rows = IMG_DEV * N_REF
    blocks = images.reshape(NIMG // group_rows, group_rows, RAD * ANG)

    def absorb(running, block):
        sums, weight_sum = running
        scores = jnp.dot(block, references.T, preferred_element_type=jnp.float32) + offsets
        top_score = jnp.max(scores, axis=1, keepdims=True)
        raised = jnp.exp(scores - top_score)
        weights = (raised / jnp.sum(raised, axis=1, keepdims=True)).astype(jnp.bfloat16)
        weight_sum = weight_sum + jnp.sum(weights.astype(jnp.float32), axis=0).reshape(K, ROT).sum(axis=1)
        shaped = weights.reshape(-1, K, ROT)
        cycles = block.reshape(-1, RAD, ANG)
        for turn_index in range(ROT):
            turned = jnp.roll(cycles, -turn_index * shift_size, axis=2).reshape(-1, RAD * ANG)
            sums = sums + jnp.dot(shaped[:, :, turn_index].T, turned, preferred_element_type=jnp.float32)
        return (sums, weight_sum), None

    start_state = (jnp.zeros((K, RAD * ANG), jnp.float32), jnp.zeros((K,), jnp.float32))
    (sums, weight_sum), unused = lax.scan(absorb, start_state, blocks)
    return sums, weight_sum
```

```python
import math
import numpy as np
import jax
import jax.numpy as jnp
from jax import lax
from jax.sharding import PartitionSpec as P

ANG = 144
ROT = 36
TURN = 4


def real_dft():
    b = np.arange(ROT)
    rows = []
    for f in range(1, ROT // 2):
        rows.append(np.cos(2 * np.pi * f * b / ROT))
        rows.append(-np.sin(2 * np.pi * f * b / ROT))
    rows = [np.ones(ROT), (-1.0) ** b] + rows
    return (np.array(rows)).astype(np.float32)


def real_idft():
    b = np.arange(ROT)
    rows = [np.ones(ROT) / ROT, (-1.0) ** b / ROT]
    for f in range(1, ROT // 2):
        rows.append(2 * np.cos(2 * np.pi * f * b / ROT) / ROT)
        rows.append(-2 * np.sin(2 * np.pi * f * b / ROT) / ROT)
    return np.array(rows).T.astype(np.float32)


def per_device(images, references, class_prior):
    hi = lax.Precision.HIGHEST
    classes_here = class_prior.shape[0]
    n_img, pixels = images.shape
    rad = pixels // ANG
    templates = references.reshape(classes_here, ROT, pixels)[:, 0]
    half_norm = 0.5 * jnp.sum(jnp.square(templates.astype(jnp.float32)), axis=1)
    offset = jnp.log(class_prior) - half_norm
    offsets = lax.all_gather(offset, "ref", axis=0, tiled=True)
    tall = lax.all_gather(templates, "ref", axis=0, tiled=True)
    k = tall.shape[0]
    dft, idft = real_dft(), real_idft()
    x5 = images.reshape(n_img, rad, ROT, TURN).transpose(2, 0, 1, 3).reshape(ROT, n_img, rad * TURN)
    t5 = tall.reshape(k, rad, ROT, TURN).transpose(2, 0, 1, 3).reshape(ROT, k, rad * TURN)
    xh = jnp.einsum("jb,bnc->jnc", dft, x5.astype(jnp.float32), precision=hi)
    th = jnp.einsum("jb,bkc->jkc", dft, t5.astype(jnp.float32), precision=hi)
    xr, xi = xh[0::2], xh[1::2]
    tr, ti = th[0::2], th[1::2]
    dot = lambda a, b: jnp.einsum("fkc,fnc->fkn", a, b, precision=hi)
    rr, ii = dot(tr, xr), dot(ti, xi)
    ri, ir = dot(tr[1:], xi[1:]), dot(ti[1:], xr[1:])
    sr = jnp.concatenate([rr[:1], rr[1:] + ii[1:]])
    si = jnp.concatenate([ii[:1], ri - ir])
    sh = jnp.stack([sr, si], axis=1).reshape(ROT, k, n_img)
    scores = jnp.einsum("rj,jkn->rkn", idft, sh, precision=hi) + offsets[None, :, None]
    top = jnp.max(scores, axis=(0, 1))
    e = jnp.exp(scores - top)
    weights = (e / jnp.sum(e, axis=(0, 1))).astype(jnp.bfloat16).astype(jnp.float32)
    mass = jnp.sum(weights, axis=(0, 2))
    class_weights = lax.psum_scatter(lax.psum(mass, "img"), "ref", scatter_dimension=0, tiled=True)
    wh = jnp.einsum("jr,rkn->jkn", dft, weights, precision=hi)
    wr, wi = wh[0::2], wh[1::2]
    dot2 = lambda a, b: jnp.einsum("fkn,fnc->fkc", a, b, precision=hi)
    cr = jnp.concatenate([dot2(wr[:1], xr[:1]), dot2(wr[1:], xr[1:]) + dot2(wi[1:], xi[1:])])
    ci = jnp.concatenate([dot2(wi[:1], xi[:1]), dot2(wr[1:], xi[1:]) - dot2(wi[1:], xr[1:])])
    c = jnp.stack([cr, ci], axis=1).reshape(ROT, k, rad, TURN)
    sums = jnp.einsum("bj,jkqc->kqbc", idft, c, precision=hi).reshape(k, pixels)
    sums = lax.psum_scatter(sums, "ref", scatter_dimension=0, tiled=True)
    class_sums = lax.psum_scatter(sums, "img", scatter_dimension=1, tiled=True)
    return (class_sums, class_weights)


def solution(mesh):
    placed = (P(("img", "ref"), None), P("ref", None), P("ref"))
    return jax.shard_map(
        per_device,
        mesh=mesh,
        in_specs=placed,
        out_specs=(P("ref", "img"), P("ref")),
        check_vma=False,
    )
```

```python
import math
import numpy as np
import jax
import jax.numpy as jnp
from jax import lax
from jax.experimental import pallas as pl
from jax.experimental.pallas import tpu as pltpu
from jax.sharding import PartitionSpec as P

ANG = 144
ROT = 36
TURN = 4
BAND = 1152
HALF = ROT // 2
F32 = jnp.float32
BF16 = jnp.bfloat16
MESH = pl.DeviceIdType.MESH

COS9 = [math.cos(2 * math.pi * m / 9) for m in range(9)]
SIN9 = [math.sin(2 * math.pi * m / 9) for m in range(9)]
ROOT3H = math.sqrt(3.0) / 2


def cos_sums(y0, e):
    t = e[0] + e[1] + e[3]
    top = y0 + e[2]
    base = y0 - 0.5 * e[2]
    out = [top + t]
    for f in (1, 2, 4):
        out.append(base + COS9[f % 9] * e[0] + COS9[2 * f % 9] * e[1] + COS9[4 * f % 9] * e[3])
    out.insert(3, top - 0.5 * t)
    return out


def sin_sums(o):
    h = ROOT3H * o[2]
    one = SIN9[1] * o[0] + SIN9[2] * o[1] + h + SIN9[4] * o[3]
    two = SIN9[2] * o[0] + SIN9[4] * o[1] - h - SIN9[1] * o[3]
    three = ROOT3H * (o[0] - o[1] + o[3])
    four = SIN9[4] * o[0] - SIN9[1] * o[1] + h - SIN9[2] * o[3]
    return [one, two, three, four]


def real9(y):
    e = [y[m] + y[9 - m] for m in range(1, 5)]
    o = [y[m] - y[9 - m] for m in range(1, 5)]
    s = sin_sums(o)
    return cos_sums(y[0], e), [None] + [-v for v in s]


def forward36(x):
    y0, y2, y1r, y1i = [], [], [], []
    for b2 in range(9):
        x0, x1, x2, x3 = (x[(9 * b1 + 4 * b2) % 36] for b1 in range(4))
        u0, u1, v0, v1 = x0 + x2, x0 - x2, x1 + x3, x3 - x1
        y0.append(u0 + v0)
        y2.append(u0 - v0)
        y1r.append(u1)
        y1i.append(v1)
    z0r, z0i = real9(y0)
    z2r, z2i = real9(y2)
    ur, ui = real9(y1r)
    vr, vi = real9(y1i)
    z1r, z1i = [None] * 9, [None] * 9
    z1r[0], z1i[0] = ur[0], vr[0]
    for f in range(1, 5):
        z1r[f], z1i[f] = ur[f] - vi[f], ui[f] + vr[f]
        z1r[9 - f], z1i[9 - f] = ur[f] + vi[f], vr[f] - ui[f]

    def at(f):
        f1, f2 = f % 4, f % 9
        if f1 in (0, 2):
            r, i = (z0r, z0i) if f1 == 0 else (z2r, z2i)
            if f2 == 0:
                return r[0], None
            return (r[f2], i[f2]) if f2 <= 4 else (r[9 - f2], -i[9 - f2])
        if f1 == 1:
            return z1r[f2], z1i[f2]
        g = (9 - f2) % 9
        return z1r[g], -z1i[g]

    return [(at(0)[0], at(18)[0])] + [at(f) for f in range(1, HALF)]


def inverse36(pairs):
    def spec(f):
        f %= 36
        if f == 0:
            return pairs[0][0], None
        if f == 18:
            return pairs[0][1], None
        if f < 18:
            return pairs[f]
        r, i = pairs[36 - f]
        return r, -i

    def find(f1, f2):
        return spec(next(f for f in range(36) if f % 4 == f1 and f % 9 == f2))

    def hermitian(f1):
        r0 = find(f1, 0)[0]
        z = [find(f1, f) for f in range(1, 5)]
        c = cos_sums(r0, [2.0 * r for r, _ in z])
        s = sin_sums([2.0 * i for _, i in z])
        y = [None] * 9
        y[0] = c[0]
        for m in range(1, 5):
            y[m], y[9 - m] = c[m] - s[m - 1], c[m] + s[m - 1]
        return y

    y0, y2 = hermitian(0), hermitian(2)
    z = [find(1, f) for f in range(9)]
    er = [z[f][0] + z[9 - f][0] for f in range(1, 5)]
    ei = [z[f][1] + z[9 - f][1] for f in range(1, 5)]
    dr = [z[f][0] - z[9 - f][0] for f in range(1, 5)]
    di = [z[f][1] - z[9 - f][1] for f in range(1, 5)]
    cr, ci = cos_sums(z[0][0], er), cos_sums(z[0][1], ei)
    sr, si = sin_sums(dr), sin_sums(di)
    y1r, y1i = [cr[0]] + [None] * 8, [ci[0]] + [None] * 8
    for m in range(1, 5):
        y1r[m], y1r[9 - m] = cr[m] - si[m - 1], cr[m] + si[m - 1]
        y1i[m], y1i[9 - m] = ci[m] + sr[m - 1], ci[m] - sr[m - 1]
    x = [None] * 36
    for b2 in range(9):
        p, q = y0[b2] + y2[b2], y0[b2] - y2[b2]
        a, b = 2.0 * y1r[b2], 2.0 * y1i[b2]
        for b1, v in enumerate((p + a, q - b, p - a, q + b)):
            x[(9 * b1 + 4 * b2) % 36] = v
    return x


def lane(shape):
    return lax.broadcasted_iota(jnp.int32, shape, len(shape) - 1)


def turn32(a):
    l = lane(a[0].shape)
    low = l < 64
    even = (l // 32) % 2 == 0
    b0 = jnp.where(low, a[0], pltpu.roll(a[2], 64, 1))
    b2 = jnp.where(low, pltpu.roll(a[0], 64, 1), a[2])
    b1 = jnp.where(low, a[1], pltpu.roll(a[3], 64, 1))
    b3 = jnp.where(low, pltpu.roll(a[1], 64, 1), a[3])
    out = []
    for p, q in ((b0, b1), (b2, b3)):
        out.append(jnp.where(even, p, pltpu.roll(q, 32, 1)))
        out.append(jnp.where(even, pltpu.roll(p, 96, 1), q))
    return out


def split(v):
    h = v.astype(BF16)
    return h, (v - h.astype(F32)).astype(BF16)


NT = (((1,), (1,)), ((), ()))
NN = (((1,), (0,)), ((), ()))


def dot(a, b, dims=NN):
    return lax.dot_general(a, b, dims, preferred_element_type=F32)


def kernel(
    prior, images, refs, perm, out,
    rows16, tload, x5, xh, tbuf, tf, tmix, offs, sh, stat, lh, mass, cf, cmix, cb, rb,
    load_sem, perm_sem, send_sem, recv_sem, off_send, off_recv, pair_send, pair_recv, rs_send, rs_recv,
):
    img, ref = lax.axis_index("img"), lax.axis_index("ref")
    z, yh = img // 2, img % 2
    x, yl, core = ref // 4, (ref // 2) % 2, ref % 2

    def dev(x_, y_, z_, c_):
        return {"img": z_ * 2 + y_ // 2, "ref": x_ * 4 + (y_ % 2) * 2 + c_}

    y = yh * 2 + yl
    xp, xm = (x + 1) % 4, (x + 3) % 4
    x2 = (x + 2) % 4
    to_xp, to_xm = dev(xp, y, z, core), dev(xm, y, z, core)
    to_yp, to_ym = dev(x, (y + 1) % 4, z, core), dev(x, (y + 3) % 4, z, core)
    sibling = dev(x, y, z, 1 - core)

    loads = []
    for k in range(12):
        c = pltpu.make_async_copy(refs.at[pl.ds(36 * k // 16 * 16, 16)], rows16.at[k], load_sem.at[k])
        c.start()
        loads.append(c)

    def away(d):
        zz, hh, xx, ll = d // 16, (d // 8) % 2, (d // 2) % 4, d % 2
        return {
            "img": ((z + zz) % 4) * 2 + (yh + hh) % 2,
            "ref": ((x + xx) % 4) * 4 + ((yl + ll) % 2) * 2 + core,
        }

    barrier = pltpu.get_barrier_semaphore()

    def greet(d, c):
        pl.semaphore_signal(barrier, inc=1, device_id=away(d), device_id_type=MESH)
        return c

    lax.fori_loop(1, 64, greet, 0)
    pl.semaphore_signal(barrier, inc=1, device_id=sibling, device_id_type=MESH)
    pl.semaphore_wait(barrier, 64)

    for c in loads:
        c.wait()
    norm = jnp.zeros((16, 128), F32)
    for g in range(8):
        tiles = []
        for k in range(12):
            at = 36 * k % 16
            tiles.append(rows16[k, :, g * BAND : (g + 1) * BAND].astype(F32)[at : at + 1])
        tiles.append(jnp.zeros((4, BAND), F32))
        t = jnp.concatenate(tiles, axis=0)
        for v in range(9):
            part = t[:, v * 128 : (v + 1) * 128]
            norm = norm + part * part
        tload[g * 16 : (g + 1) * 16, :] = t.astype(BF16)
    half_norm = 0.5 * jnp.sum(norm, axis=1, keepdims=True)
    rowid = lax.broadcasted_iota(jnp.int32, (16, 128), 0)
    pri = jnp.ones((16, 128), F32)
    for k in range(12):
        pri = jnp.where(rowid == k, prior[k], pri)
    slot = x * 2 + yl
    offs[slot] = jnp.log(pri) - half_norm

    sub8 = lax.broadcasted_iota(jnp.int32, (8, 128), 0)

    def arrange(v, c):
        o = dot(tload[...], perm[:, pl.ds(pl.multiple_of(v * 128, 128), 128)])
        halves = [turn32([o[(2 * zz + h) * 16 : (2 * zz + h) * 16 + 16] for zz in range(4)]) for h in range(2)]
        rows = []
        for i in range(4):
            a, b = halves[0][i], halves[1][i]
            rows += [a[:8], b[:8], jnp.where(sub8 < 4, a[8:], pltpu.roll(b[8:], 4, 0))]
        tbuf[slot, pl.ds(pl.multiple_of(96 * v, 32), 96), :] = jnp.concatenate(rows, axis=0).astype(BF16)
        return c

    lax.fori_loop(0, 9, arrange, 0)

    def piece(s, half):
        return tbuf.at[s, pl.ds(432 * half, 432)]

    started = []

    def send(s, half, target, n):
        c = pltpu.make_async_remote_copy(
            piece(s, half), piece(s, half), send_sem.at[n], recv_sem.at[n], device_id=target, device_id_type=MESH
        )
        c.start()
        started.append(c)

    def arrived(s, half, n):
        pltpu.make_async_copy(piece(s, half), piece(s, half), recv_sem.at[n]).wait()

    send(slot, 0, to_xp, 0)
    send(slot, 1, to_xm, 2)
    send(slot, 0, to_yp, 6)
    send(slot, 1, to_ym, 7)
    send(slot, 1, to_xp, 1)
    send(slot, 0, to_xm, 3)
    off_copies = []
    for d in range(1, 8):
        c = pltpu.make_async_remote_copy(
            offs.at[slot], offs.at[slot], off_send.at[d], off_recv.at[d], device_id=away(d), device_id_type=MESH
        )
        c.start()
        off_copies.append(c)
    s_m, s_p, s_2 = xm * 2 + yl, xp * 2 + yl, x2 * 2 + yl
    o_0, o_m, o_p, o_2 = x * 2 + 1 - yl, xm * 2 + 1 - yl, xp * 2 + 1 - yl, x2 * 2 + 1 - yl

    for g in range(3):
        cols = slice(g * 384, g * 384 + 384)
        parts = [dot(images[:, q * BAND : (q + 1) * BAND], perm[:, cols]) for q in range(8)]
        for vv in range(3):
            v = 3 * g + vv
            for h in range(2):
                t = turn32([parts[2 * zz + h][:, vv * 128 : vv * 128 + 128] for zz in range(4)])
                for i in range(4):
                    x5[core, 4 * v + i, :, h * 128 : h * 128 + 128] = t[i].astype(BF16)
    swap = pltpu.make_async_remote_copy(
        x5.at[core], x5.at[core], pair_send.at[0], pair_recv.at[0], device_id=sibling, device_id_type=MESH
    )
    swap.start()

    arrived(s_m, 0, 0)
    send(s_m, 0, to_xp, 4)
    send(s_m, 0, to_yp, 8)
    arrived(s_p, 1, 2)
    send(s_p, 1, to_xm, 5)
    send(s_p, 1, to_ym, 9)

    def image_spectra(c):
        def step(n, carry):
            t, h = n // 2, n % 2
            r0 = pl.multiple_of(t * 16, 16)
            lanes = pl.ds(pl.multiple_of(h * 128, 128), 128)
            p = forward36([x5[c, b, pl.ds(r0, 16), lanes].astype(F32) for b in range(36)])
            for f in range(HALF):
                for ri in range(2):
                    a, b = split(p[f][ri])
                    at = pl.ds(pl.multiple_of(ri * 128 + c * 64 + r0, 16), 16)
                    xh[f, 0, at, lanes] = a
                    xh[f, 1, at, lanes] = b
            return carry

        lax.fori_loop(0, 8, step, 0)

    image_spectra(core)
    arrived(s_p, 0, 3)
    send(s_p, 0, to_yp, 10)
    arrived(s_m, 1, 1)
    send(s_m, 1, to_ym, 11)
    swap.wait()
    image_spectra(1 - core)
    arrived(s_2, 0, 4)
    send(s_2, 0, to_yp, 12)
    arrived(s_2, 1, 5)
    send(s_2, 1, to_ym, 13)

    def template_spectra(xx, ll):
        s = xx * 2 + ll
        raw = []
        for b in range(HALF):
            two = tbuf[s, 48 * b : 48 * b + 48, :].astype(F32)
            raw += [two[:24], two[24:]]
        p = forward36(raw)
        at = pl.ds(pl.multiple_of(ll * 32 + xx * 8, 8), 8)
        for f in range(HALF):
            for ri in range(2):
                v = p[f][ri]
                tf[f, ri, at, 0:128] = v[0:8]
                tf[f, ri, at, 128:256] = v[8:16]
                tmix[s, f, ri] = v[16:24]

    def own_row(n, c):
        template_spectra((x + n) % 4, yl)
        return c

    lax.fori_loop(0, 4, own_row, 0)
    arrived(o_0, 0, 6)
    arrived(o_0, 1, 7)
    arrived(o_m, 0, 8)
    arrived(o_p, 1, 9)
    arrived(o_p, 0, 10)
    arrived(o_m, 1, 11)
    arrived(o_2, 0, 12)
    arrived(o_2, 1, 13)

    def other_row(n, c):
        template_spectra((x + n) % 4, 1 - yl)
        return c

    lax.fori_loop(0, 4, other_row, 0)
    for c in off_copies:
        c.wait()

    def score(f, c):
        for ri in range(2):
            mix = [tmix[s, f, ri] for s in range(8)]
            for xx in range(4):
                a, b = mix[2 * xx], mix[2 * xx + 1]
                tf[f, ri, 64 + 8 * xx : 72 + 8 * xx, 0:128] = jnp.where(sub8 < 4, a, pltpu.roll(b, 4, 0))
                tf[f, ri, 64 + 8 * xx : 72 + 8 * xx, 128:256] = jnp.where(sub8 < 4, pltpu.roll(a, 4, 0), b)
        rh, rl = split(tf[f, 0])
        ih, il = split(tf[f, 1])
        high = jnp.concatenate([rh, ih], axis=0)
        low = jnp.concatenate([rl, il], axis=0)
        m = dot(high, xh[f, 0], NT) + (dot(low, xh[f, 0], NT) + dot(high, xh[f, 1], NT))
        rr, ri_, ir, ii = m[:96, :128], m[:96, 128:], m[96:, :128], m[96:, 128:]
        first = f == 0
        sh[2 * f] = jnp.where(first, rr, rr + ii)
        sh[2 * f + 1] = jnp.where(first, ii, ri_ - ir)
        return c

    lax.fori_loop(0, HALF, score, 0)

    def to_turns(xx, off, rows, top):
        p = [(sh[2 * f, rows, :], sh[2 * f + 1, rows, :]) for f in range(HALF)]
        s = inverse36(p)
        for r in range(36):
            v = s[r] * (1.0 / 36.0) + off
            sh[r, rows, :] = v
            top = jnp.maximum(top, v)
        return top

    def rows_of(n, c):
        lo, hi = n % 4, n // 4
        plain = offs[lo * 2 + jnp.minimum(hi, 1)]
        a, b = offs[lo * 2], offs[lo * 2 + 1]
        last = jnp.where(sub8 < 4, a[8:], pltpu.roll(b[8:], 4, 0))
        off = jnp.where(hi == 2, last, plain[:8])
        return to_turns(lo, off, pl.ds(pl.multiple_of(n * 8, 8), 8), c)

    top8 = lax.fori_loop(0, 12, rows_of, jnp.full((8, 128), -jnp.inf, F32))
    top = jnp.max(top8, axis=0, keepdims=True)

    def raise_(n, c):
        rows = pl.ds(pl.multiple_of(n * 8, 8), 8)
        for r in range(36):
            e = jnp.exp(sh[r, rows, :] - top)
            sh[r, rows, :] = e
            c = c + e
        return c

    total = jnp.sum(lax.fori_loop(0, 12, raise_, jnp.zeros((8, 128), F32)), axis=0, keepdims=True)
    stat[0, 0] = jnp.broadcast_to(top, (8, 128))
    stat[0, 1] = jnp.broadcast_to(total, (8, 128))
    share = pltpu.make_async_remote_copy(
        stat.at[0], stat.at[1], pair_send.at[1], pair_recv.at[1], device_id=sibling, device_id_type=MESH
    )
    share.start()
    share.wait()
    top_o, total_o = stat[1, 0][:1], stat[1, 1][:1]
    peak = jnp.maximum(top, top_o)
    mine = jnp.exp(top - peak)
    scale = mine / (total * mine + total_o * jnp.exp(top_o - peak))

    def weigh(n, c):
        rows = pl.ds(pl.multiple_of(n * 16, 16), 16)
        upper = pl.ds(pl.multiple_of(n * 16 + 96, 16), 16)
        w = [(sh[r, rows, :] * scale).astype(BF16).astype(F32) for r in range(36)]
        p = forward36(w)
        mass[rows, :] = jnp.broadcast_to(jnp.sum(p[0][0], axis=1, keepdims=True), (16, 128))
        none = jnp.zeros((16, 128), BF16)
        for f in range(HALF):
            for part, (r, i) in enumerate(zip(split(p[f][0]), split(p[f][1]))):
                lh[f, part, rows, 0:128] = r
                lh[f, part, rows, 128:256] = none if f == 0 else i
                lh[f, part, upper, 0:128] = none if f == 0 else -i
                lh[f, part, upper, 128:256] = i if f == 0 else r
        return c

    lax.fori_loop(0, 6, weigh, 0)

    def sums(u, c):
        comps = []
        for ff in range(2):
            f = 2 * u + ff
            a, b = lh[f, 0], lh[f, 1]
            m = dot(a, xh[f, 0]) + (dot(b, xh[f, 0]) + dot(a, xh[f, 1]))
            comps += [m[:96], m[96:]]
        at = pl.ds(pl.multiple_of(8 * u, 8), 8)
        for h in range(2):
            t = turn32([v[:, h * 128 : h * 128 + 128] for v in comps])
            for zz in range(4):
                for xx in range(4):
                    cf[zz, h, xx, 0, at, :] = t[zz][8 * xx : 8 * xx + 8]
                    cf[zz, h, xx, 1, at, :] = t[zz][32 + 8 * xx : 40 + 8 * xx]
                    cmix[zz, h, xx, u] = t[zz][64 + 8 * xx : 72 + 8 * xx]
        return c

    lax.fori_loop(0, 9, sums, 0)

    l8 = lane((8, 128)) // 16

    def pack(zz, hh, xx):
        mixes = [cmix[zz, hh, xx, u] for u in range(9)]
        tail0, tail1 = [], []
        for u in range(0, 8, 2):
            a, b = mixes[u], mixes[u + 1]
            tail0.append(jnp.where(sub8 < 4, a, pltpu.roll(b, 4, 0)))
            tail1.append(jnp.where(sub8 < 4, pltpu.roll(a, 4, 0), b))
        mm = mass[pl.ds(pl.multiple_of(64 + 8 * xx, 8), 8), :]
        m0 = mass[pl.ds(pl.multiple_of(8 * xx, 8), 8), :]
        m1 = mass[pl.ds(pl.multiple_of(32 + 8 * xx, 8), 8), :]
        for ll, (m8, m4, last) in enumerate(
            ((m0, pltpu.roll(mm, 4, 0), mixes[8]), (m1, mm, pltpu.roll(mixes[8], 4, 0)))
        ):
            v = jnp.where(l8 < 2, pltpu.roll(m8, 4, 0), jnp.where(l8 < 4, m8, m4))
            vh = v.astype(BF16).astype(F32)
            v = jnp.where(l8 % 2 == 0, vh, v - vh)
            (tail0, tail1)[ll].append(jnp.where(sub8 < 4, last, v))
        for ll, tail in enumerate((tail0, tail1)):
            cb[zz, hh, xx, ll] = jnp.concatenate(
                [cf[zz, hh, xx, ll, 0:72, :]] + tail, axis=0
            ).astype(BF16)

    def pack_step(n, c):
        pack(n // 8, (n // 4) % 2, n % 4)
        return c

    lax.fori_loop(0, 32, pack_step, 0)

    def scatter_copy(d):
        zz, hh, xx, ll = (z + d // 16) % 4, (yh + d // 8) % 2, (x + (d // 2) % 4) % 4, (yl + d) % 2
        return pltpu.make_async_remote_copy(
            cb.at[zz, hh, xx, ll], rb.at[d], rs_send.at[d], rs_recv.at[d], device_id=away(d), device_id_type=MESH
        )

    def scatter(d, c):
        scatter_copy(d).start()
        return c

    lax.fori_loop(1, 64, scatter, 0)
    acc = cb[z, yh, x, yl].astype(F32)

    def gather(d, acc):
        scatter_copy(d).wait_recv()
        return acc + rb[d].astype(F32)

    out[...] = lax.fori_loop(1, 64, gather, acc)

    def finish(d, c):
        scatter_copy(d).wait_send()
        return c

    lax.fori_loop(1, 64, finish, 0)
    for c in started:
        c.wait_send()


def column_order():
    q, b, c = np.meshgrid(np.arange(8), np.arange(ROT), np.arange(TURN), indexing="ij")
    perm = np.zeros((BAND, BAND), np.float32)
    perm[(q * ANG + b * TURN + c).ravel(), (b * 32 + q * 4 + c).ravel()] = 1
    return perm


def real_idft():
    b = np.arange(ROT)
    rows = [np.ones(ROT) / ROT, (-1.0) ** b / ROT]
    for f in range(1, HALF):
        rows.append(2 * np.cos(2 * np.pi * f * b / ROT) / ROT)
        rows.append(-2 * np.sin(2 * np.pi * f * b / ROT) / ROT)
    return np.array(rows).astype(np.float32).reshape(9, 4, ROT)


def per_device(images, references, class_prior):
    perm = jnp.asarray(column_order(), BF16)
    vmem = pl.BlockSpec(memory_space=pltpu.VMEM)
    v = pl.pallas_call(
        kernel,
        out_shape=jax.ShapeDtypeStruct((112, 128), F32),
        in_specs=[
            pl.BlockSpec(memory_space=pltpu.SMEM),
            vmem,
            pl.BlockSpec(memory_space=pl.ANY),
            vmem,
        ],
        out_specs=vmem,
        scratch_shapes=[
            pltpu.VMEM((12, 16, 9216), BF16),
            pltpu.VMEM((128, BAND), BF16),
            pltpu.VMEM((2, 36, 64, 256), BF16),
            pltpu.VMEM((HALF, 2, 256, 256), BF16),
            pltpu.VMEM((8, 864, 128), BF16),
            pltpu.VMEM((HALF, 2, 96, 256), F32),
            pltpu.VMEM((8, HALF, 2, 8, 128), F32),
            pltpu.VMEM((8, 16, 128), F32),
            pltpu.VMEM((36, 96, 128), F32),
            pltpu.VMEM((2, 2, 8, 128), F32),
            pltpu.VMEM((HALF, 2, 192, 256), BF16),
            pltpu.VMEM((96, 128), F32),
            pltpu.VMEM((4, 2, 4, 2, 72, 128), F32),
            pltpu.VMEM((4, 2, 4, 9, 8, 128), F32),
            pltpu.VMEM((4, 2, 4, 2, 112, 128), BF16),
            pltpu.VMEM((64, 112, 128), BF16),
            pltpu.SemaphoreType.DMA((12,)),
            pltpu.SemaphoreType.DMA((1,)),
            pltpu.SemaphoreType.DMA((14,)),
            pltpu.SemaphoreType.DMA((14,)),
            pltpu.SemaphoreType.DMA((8,)),
            pltpu.SemaphoreType.DMA((8,)),
            pltpu.SemaphoreType.DMA((2,)),
            pltpu.SemaphoreType.DMA((2,)),
            pltpu.SemaphoreType.DMA((64,)),
            pltpu.SemaphoreType.DMA((64,)),
        ],
        compiler_params=pltpu.CompilerParams(
            collective_id=0, has_side_effects=True, vmem_limit_bytes=56 * 1024 * 1024
        ),
        name="em_pass",
    )(class_prior, images, references, perm)
    low = v[:72].reshape(9, 8, 4, 8, TURN)
    high = v[72:108].reshape(9, 4, 4, 8, TURN)
    val = jnp.concatenate([low, high], axis=1)
    sums = jnp.einsum("ukiqc,uib->kqbc", val, real_idft(), precision=lax.Precision.HIGHEST)
    m = v[108:112].reshape(4, 8, 16)[:, :6, 0].reshape(4, 3, 2)
    class_weights = jnp.sum(m, axis=2).T.reshape(12)
    return (sums.reshape(12, BAND), class_weights)


def solution(mesh):
    placed = (P(("img", "ref"), None), P("ref", None), P("ref"))
    return jax.shard_map(
        per_device,
        mesh=mesh,
        in_specs=placed,
        out_specs=(P("ref", "img"), P("ref")),
        check_vma=False,
    )
```

```python
import math
import numpy as np
import jax
import jax.numpy as jnp
from jax import lax
from jax.experimental import pallas as pl
from jax.experimental.pallas import tpu as pltpu
from jax.sharding import PartitionSpec as P

ANG = 144
ROT = 36
TURN = 4
BAND = 1152
HALF = ROT // 2
F32 = jnp.float32
BF16 = jnp.bfloat16
MESH = pl.DeviceIdType.MESH

COS9 = [math.cos(2 * math.pi * m / 9) for m in range(9)]
SIN9 = [math.sin(2 * math.pi * m / 9) for m in range(9)]
ROOT3H = math.sqrt(3.0) / 2


def cos_sums(y0, e):
    t = e[0] + e[1] + e[3]
    top = y0 + e[2]
    base = y0 - 0.5 * e[2]
    out = [top + t]
    for f in (1, 2, 4):
        out.append(base + COS9[f % 9] * e[0] + COS9[2 * f % 9] * e[1] + COS9[4 * f % 9] * e[3])
    out.insert(3, top - 0.5 * t)
    return out


def sin_sums(o):
    h = ROOT3H * o[2]
    one = SIN9[1] * o[0] + SIN9[2] * o[1] + h + SIN9[4] * o[3]
    two = SIN9[2] * o[0] + SIN9[4] * o[1] - h - SIN9[1] * o[3]
    three = ROOT3H * (o[0] - o[1] + o[3])
    four = SIN9[4] * o[0] - SIN9[1] * o[1] + h - SIN9[2] * o[3]
    return [one, two, three, four]


def real9(y):
    e = [y[m] + y[9 - m] for m in range(1, 5)]
    o = [y[m] - y[9 - m] for m in range(1, 5)]
    s = sin_sums(o)
    return cos_sums(y[0], e), [None] + [-v for v in s]


def forward36(x):
    y0, y2, y1r, y1i = [], [], [], []
    for b2 in range(9):
        x0, x1, x2, x3 = (x[(9 * b1 + 4 * b2) % 36] for b1 in range(4))
        u0, u1, v0, v1 = x0 + x2, x0 - x2, x1 + x3, x3 - x1
        y0.append(u0 + v0)
        y2.append(u0 - v0)
        y1r.append(u1)
        y1i.append(v1)
    z0r, z0i = real9(y0)
    z2r, z2i = real9(y2)
    ur, ui = real9(y1r)
    vr, vi = real9(y1i)
    z1r, z1i = [None] * 9, [None] * 9
    z1r[0], z1i[0] = ur[0], vr[0]
    for f in range(1, 5):
        z1r[f], z1i[f] = ur[f] - vi[f], ui[f] + vr[f]
        z1r[9 - f], z1i[9 - f] = ur[f] + vi[f], vr[f] - ui[f]

    def at(f):
        f1, f2 = f % 4, f % 9
        if f1 in (0, 2):
            r, i = (z0r, z0i) if f1 == 0 else (z2r, z2i)
            if f2 == 0:
                return r[0], None
            return (r[f2], i[f2]) if f2 <= 4 else (r[9 - f2], -i[9 - f2])
        if f1 == 1:
            return z1r[f2], z1i[f2]
        g = (9 - f2) % 9
        return z1r[g], -z1i[g]

    return [(at(0)[0], at(18)[0])] + [at(f) for f in range(1, HALF)]


def inverse36(pairs):
    def spec(f):
        f %= 36
        if f == 0:
            return pairs[0][0], None
        if f == 18:
            return pairs[0][1], None
        if f < 18:
            return pairs[f]
        r, i = pairs[36 - f]
        return r, -i

    def find(f1, f2):
        return spec(next(f for f in range(36) if f % 4 == f1 and f % 9 == f2))

    def hermitian(f1):
        r0 = find(f1, 0)[0]
        z = [find(f1, f) for f in range(1, 5)]
        c = cos_sums(r0, [2.0 * r for r, _ in z])
        s = sin_sums([2.0 * i for _, i in z])
        y = [None] * 9
        y[0] = c[0]
        for m in range(1, 5):
            y[m], y[9 - m] = c[m] - s[m - 1], c[m] + s[m - 1]
        return y

    y0, y2 = hermitian(0), hermitian(2)
    z = [find(1, f) for f in range(9)]
    er = [z[f][0] + z[9 - f][0] for f in range(1, 5)]
    ei = [z[f][1] + z[9 - f][1] for f in range(1, 5)]
    dr = [z[f][0] - z[9 - f][0] for f in range(1, 5)]
    di = [z[f][1] - z[9 - f][1] for f in range(1, 5)]
    cr, ci = cos_sums(z[0][0], er), cos_sums(z[0][1], ei)
    sr, si = sin_sums(dr), sin_sums(di)
    y1r, y1i = [cr[0]] + [None] * 8, [ci[0]] + [None] * 8
    for m in range(1, 5):
        y1r[m], y1r[9 - m] = cr[m] - si[m - 1], cr[m] + si[m - 1]
        y1i[m], y1i[9 - m] = ci[m] + sr[m - 1], ci[m] - sr[m - 1]
    x = [None] * 36
    for b2 in range(9):
        p, q = y0[b2] + y2[b2], y0[b2] - y2[b2]
        a, b = 2.0 * y1r[b2], 2.0 * y1i[b2]
        for b1, v in enumerate((p + a, q - b, p - a, q + b)):
            x[(9 * b1 + 4 * b2) % 36] = v
    return x


def lane(shape):
    return lax.broadcasted_iota(jnp.int32, shape, len(shape) - 1)


def turn32(a):
    l = lane(a[0].shape)
    low = l < 64
    even = (l // 32) % 2 == 0
    b0 = jnp.where(low, a[0], pltpu.roll(a[2], 64, 1))
    b2 = jnp.where(low, pltpu.roll(a[0], 64, 1), a[2])
    b1 = jnp.where(low, a[1], pltpu.roll(a[3], 64, 1))
    b3 = jnp.where(low, pltpu.roll(a[1], 64, 1), a[3])
    out = []
    for p, q in ((b0, b1), (b2, b3)):
        out.append(jnp.where(even, p, pltpu.roll(q, 32, 1)))
        out.append(jnp.where(even, pltpu.roll(p, 96, 1), q))
    return out


def split(v):
    h = v.astype(BF16)
    return h, (v - h.astype(F32)).astype(BF16)


NT = (((1,), (1,)), ((), ()))
NN = (((1,), (0,)), ((), ()))


def dot(a, b, dims=NN):
    return lax.dot_general(a, b, dims, preferred_element_type=F32)


def kernel(
    prior, images_hbm, refs, perm_hbm, out, out_mass,
    images, perm, rows16, tload, x5, xh, tbuf, tf, tmix, offs, sh, stat, lh, mass, cf, cmix,
    own_a, own_b, own_c, s1a, s1b, s1c, r1a, r1b, r1c, s2a, s2b, s2c, r2a, r2b, r2c, s3a, s3b, s3c, r3a, r3b, r3c,
    load_sem, send_sem, recv_sem, off_send, off_recv, pair_send, pair_recv, rs_send, rs_recv,
):
    img, ref = lax.axis_index("img"), lax.axis_index("ref")
    z, yh = img // 2, img % 2
    x, yl, core = ref // 4, (ref // 2) % 2, ref % 2

    def dev(x_, y_, z_, c_):
        return {"img": z_ * 2 + y_ // 2, "ref": x_ * 4 + (y_ % 2) * 2 + c_}

    y = yh * 2 + yl
    xp, xm = (x + 1) % 4, (x + 3) % 4
    x2 = (x + 2) % 4
    to_xp, to_xm = dev(xp, y, z, core), dev(xm, y, z, core)
    to_yp, to_ym = dev(x, (y + 1) % 4, z, core), dev(x, (y + 3) % 4, z, core)
    sibling = dev(x, y, z, 1 - core)

    loads = []
    for k in range(12):
        c = pltpu.make_async_copy(refs.at[pl.ds(36 * k // 16 * 16, 16)], rows16.at[k], load_sem.at[k])
        c.start()
        loads.append(c)
    load_perm = pltpu.make_async_copy(perm_hbm, perm, load_sem.at[12])
    load_perm.start()
    load_images = pltpu.make_async_copy(images_hbm, images, load_sem.at[13])
    load_images.start()

    def along(axis, r):
        x_, y_, z_ = ((v + r * (a == axis)) % 4 for a, v in enumerate((x, y, z)))
        return dev(x_, y_, z_, core)

    def away(d):
        return dev((x + d // 2) % 4, yh * 2 + (yl + d) % 2, z, core)

    barrier = pltpu.get_barrier_semaphore()
    partners = [along(a, r) for a in range(3) for r in range(1, 4)] + [away(d) for d in (3, 5, 7)] + [sibling]
    for p in partners:
        pl.semaphore_signal(barrier, inc=1, device_id=p, device_id_type=MESH)
    pl.semaphore_wait(barrier, len(partners))

    for c in loads:
        c.wait()
    norm = jnp.zeros((16, 128), F32)
    for g in range(8):
        tiles = []
        for k in range(12):
            at = 36 * k % 16
            tiles.append(rows16[k, :, g * BAND : (g + 1) * BAND].astype(F32)[at : at + 1])
        tiles.append(jnp.zeros((4, BAND), F32))
        t = jnp.concatenate(tiles, axis=0)
        for v in range(9):
            part = t[:, v * 128 : (v + 1) * 128]
            norm = norm + part * part
        tload[g * 16 : (g + 1) * 16, :] = t.astype(BF16)
    half_norm = 0.5 * jnp.sum(norm, axis=1, keepdims=True)
    rowid = lax.broadcasted_iota(jnp.int32, (16, 128), 0)
    pri = jnp.ones((16, 128), F32)
    for k in range(12):
        pri = jnp.where(rowid == k, prior[k], pri)
    slot = x * 2 + yl
    offs[slot] = jnp.log(pri) - half_norm

    sub8 = lax.broadcasted_iota(jnp.int32, (8, 128), 0)

    load_perm.wait()

    def arrange(v, c):
        o = dot(tload[...], perm[:, pl.ds(pl.multiple_of(v * 128, 128), 128)])
        halves = [turn32([o[(2 * zz + h) * 16 : (2 * zz + h) * 16 + 16] for zz in range(4)]) for h in range(2)]
        rows = []
        for i in range(4):
            a, b = halves[0][i], halves[1][i]
            rows += [a[:8], b[:8], jnp.where(sub8 < 4, a[8:], pltpu.roll(b[8:], 4, 0))]
        tbuf[slot, pl.ds(pl.multiple_of(96 * v, 32), 96), :] = jnp.concatenate(rows, axis=0).astype(BF16)
        return c

    lax.fori_loop(0, 9, arrange, 0, unroll=9)

    def piece(s, half):
        return tbuf.at[s, pl.ds(432 * half, 432)]

    started = []

    def send(s, half, target, n):
        c = pltpu.make_async_remote_copy(
            piece(s, half), piece(s, half), send_sem.at[n], recv_sem.at[n], device_id=target, device_id_type=MESH
        )
        c.start()
        started.append(c)

    def arrived(s, half, n):
        pltpu.make_async_copy(piece(s, half), piece(s, half), recv_sem.at[n]).wait()

    send(slot, 0, to_xp, 0)
    send(slot, 1, to_xm, 2)
    send(slot, 0, to_yp, 6)
    send(slot, 1, to_ym, 7)
    send(slot, 1, to_xp, 1)
    send(slot, 0, to_xm, 3)
    off_copies = []
    for d in range(1, 8):
        c = pltpu.make_async_remote_copy(
            offs.at[slot], offs.at[slot], off_send.at[d], off_recv.at[d], device_id=away(d), device_id_type=MESH
        )
        c.start()
        off_copies.append(c)
    s_m, s_p, s_2 = xm * 2 + yl, xp * 2 + yl, x2 * 2 + yl
    o_0, o_m, o_p, o_2 = x * 2 + 1 - yl, xm * 2 + 1 - yl, xp * 2 + 1 - yl, x2 * 2 + 1 - yl

    load_images.wait()
    for g in range(3):
        cols = slice(g * 384, g * 384 + 384)
        stacked = jnp.concatenate([images[:, q * BAND : (q + 1) * BAND] for q in range(8)], axis=0)
        o = dot(stacked, perm[:, cols])
        parts = [o[q * 64 : q * 64 + 64] for q in range(8)]
        for vv in range(3):
            v = 3 * g + vv
            for h in range(2):
                t = turn32([parts[2 * zz + h][:, vv * 128 : vv * 128 + 128] for zz in range(4)])
                for i in range(4):
                    x5[core, 4 * v + i, :, h * 128 : h * 128 + 128] = t[i].astype(BF16)
    swap = pltpu.make_async_remote_copy(
        x5.at[core], x5.at[core], pair_send.at[0], pair_recv.at[0], device_id=sibling, device_id_type=MESH
    )
    swap.start()

    arrived(s_m, 0, 0)
    send(s_m, 0, to_xp, 4)
    send(s_m, 0, to_yp, 8)
    arrived(s_p, 1, 2)
    send(s_p, 1, to_xm, 5)
    send(s_p, 1, to_ym, 9)

    def image_spectra(c):
        def step(n, carry):
            t, h = n // 2, n % 2
            r0 = pl.multiple_of(t * 16, 16)
            lanes = pl.ds(pl.multiple_of(h * 128, 128), 128)
            p = forward36([x5[c, b, pl.ds(r0, 16), lanes].astype(F32) for b in range(36)])
            for f in range(HALF):
                for ri in range(2):
                    a, b = split(p[f][ri])
                    at = pl.ds(pl.multiple_of(ri * 128 + c * 64 + r0, 16), 16)
                    xh[f, 0, at, lanes] = a
                    xh[f, 1, at, lanes] = b
            return carry

        lax.fori_loop(0, 8, step, 0)

    image_spectra(core)
    arrived(s_p, 0, 3)
    send(s_p, 0, to_yp, 10)
    arrived(s_m, 1, 1)
    send(s_m, 1, to_ym, 11)
    swap.wait()
    image_spectra(1 - core)
    arrived(s_2, 0, 4)
    send(s_2, 0, to_yp, 12)
    arrived(s_2, 1, 5)
    send(s_2, 1, to_ym, 13)

    def template_spectra(xx, ll):
        s = xx * 2 + ll
        raw = []
        for b in range(HALF):
            two = tbuf[s, 48 * b : 48 * b + 48, :].astype(F32)
            raw += [two[:24], two[24:]]
        p = forward36(raw)
        at = pl.ds(pl.multiple_of(ll * 32 + xx * 8, 8), 8)
        for f in range(HALF):
            for ri in range(2):
                v = p[f][ri]
                tf[f, ri, at, 0:128] = v[0:8]
                tf[f, ri, at, 128:256] = v[8:16]
                tmix[s, f, ri] = v[16:24]

    def own_row(n, c):
        template_spectra((x + n) % 4, yl)
        return c

    lax.fori_loop(0, 4, own_row, 0)
    arrived(o_0, 0, 6)
    arrived(o_0, 1, 7)
    arrived(o_m, 0, 8)
    arrived(o_p, 1, 9)
    arrived(o_p, 0, 10)
    arrived(o_m, 1, 11)
    arrived(o_2, 0, 12)
    arrived(o_2, 1, 13)

    def other_row(n, c):
        template_spectra((x + n) % 4, 1 - yl)
        return c

    lax.fori_loop(0, 4, other_row, 0)
    for c in off_copies:
        c.wait()

    def score(f, c):
        for ri in range(2):
            mix = [tmix[s, f, ri] for s in range(8)]
            for xx in range(4):
                a, b = mix[2 * xx], mix[2 * xx + 1]
                tf[f, ri, 64 + 8 * xx : 72 + 8 * xx, 0:128] = jnp.where(sub8 < 4, a, pltpu.roll(b, 4, 0))
                tf[f, ri, 64 + 8 * xx : 72 + 8 * xx, 128:256] = jnp.where(sub8 < 4, pltpu.roll(a, 4, 0), b)
        rh, rl = split(tf[f, 0])
        ih, il = split(tf[f, 1])
        high = jnp.concatenate([rh, ih], axis=0)
        low = jnp.concatenate([rl, il], axis=0)
        m = dot(high, xh[f, 0], NT) + (dot(low, xh[f, 0], NT) + dot(high, xh[f, 1], NT))
        rr, ri_, ir, ii = m[:96, :128], m[:96, 128:], m[96:, :128], m[96:, 128:]
        first = f == 0
        sh[2 * f] = jnp.where(first, rr, rr + ii)
        sh[2 * f + 1] = jnp.where(first, ii, ri_ - ir)
        return c

    lax.fori_loop(0, HALF, score, 0, unroll=6)

    def to_turns(xx, off, rows, top):
        p = [(sh[2 * f, rows, :], sh[2 * f + 1, rows, :]) for f in range(HALF)]
        s = inverse36(p)
        for r in range(36):
            v = s[r] * (1.0 / 36.0) + off
            sh[r, rows, :] = v
            top = jnp.maximum(top, v)
        return top

    def rows_of(n, c):
        lo, hi = n % 4, n // 4
        plain = offs[lo * 2 + jnp.minimum(hi, 1)]
        a, b = offs[lo * 2], offs[lo * 2 + 1]
        last = jnp.where(sub8 < 4, a[8:], pltpu.roll(b[8:], 4, 0))
        off = jnp.where(hi == 2, last, plain[:8])
        return to_turns(lo, off, pl.ds(pl.multiple_of(n * 8, 8), 8), c)

    top8 = lax.fori_loop(0, 12, rows_of, jnp.full((8, 128), -jnp.inf, F32))
    top = jnp.max(top8, axis=0, keepdims=True)

    def raise_(n, c):
        rows = pl.ds(pl.multiple_of(n * 8, 8), 8)
        for r in range(36):
            e = jnp.exp(sh[r, rows, :] - top)
            sh[r, rows, :] = e
            c = c + e
        return c

    total = jnp.sum(lax.fori_loop(0, 12, raise_, jnp.zeros((8, 128), F32)), axis=0, keepdims=True)
    stat[0, 0] = jnp.broadcast_to(top, (8, 128))
    stat[0, 1] = jnp.broadcast_to(total, (8, 128))
    share = pltpu.make_async_remote_copy(
        stat.at[0], stat.at[1], pair_send.at[1], pair_recv.at[1], device_id=sibling, device_id_type=MESH
    )
    share.start()
    share.wait()
    top_o, total_o = stat[1, 0][:1], stat[1, 1][:1]
    peak = jnp.maximum(top, top_o)
    mine = jnp.exp(top - peak)
    scale = mine / (total * mine + total_o * jnp.exp(top_o - peak))

    def weigh(n, c):
        rows = pl.ds(pl.multiple_of(n * 16, 16), 16)
        upper = pl.ds(pl.multiple_of(n * 16 + 96, 16), 16)
        w = [(sh[r, rows, :] * scale).astype(BF16).astype(F32) for r in range(36)]
        p = forward36(w)
        mass[rows, :] = jnp.broadcast_to(jnp.sum(p[0][0], axis=1, keepdims=True), (16, 128))
        none = jnp.zeros((16, 128), BF16)
        for f in range(HALF):
            for part, (r, i) in enumerate(zip(split(p[f][0]), split(p[f][1]))):
                lh[f, part, rows, 0:128] = r
                lh[f, part, rows, 128:256] = none if f == 0 else i
                lh[f, part, upper, 0:128] = none if f == 0 else -i
                lh[f, part, upper, 128:256] = i if f == 0 else r
        return c

    lax.fori_loop(0, 6, weigh, 0)

    def sums(u, c):
        comps = []
        for ff in range(2):
            f = 2 * u + ff
            a, b = lh[f, 0], lh[f, 1]
            m = dot(a, xh[f, 0]) + (dot(b, xh[f, 0]) + dot(a, xh[f, 1]))
            comps += [m[:96], m[96:]]
        at = pl.ds(pl.multiple_of(8 * u, 8), 8)
        for h in range(2):
            t = turn32([v[:, h * 128 : h * 128 + 128] for v in comps])
            for zz in range(4):
                for xx in range(4):
                    cf[zz, h, xx, 0, at, :] = t[zz][8 * xx : 8 * xx + 8]
                    cf[zz, h, xx, 1, at, :] = t[zz][32 + 8 * xx : 40 + 8 * xx]
                    cmix[zz, h, xx, u] = t[zz][64 + 8 * xx : 72 + 8 * xx]
        return c

    place = (x, y, z)
    copies = []

    def stage(n, axis, src, dst):
        group = []
        for r in range(1, 4):
            c = pltpu.make_async_remote_copy(
                src.at[(place[axis] + r) % 4], dst.at[r],
                rs_send.at[3 * n + r - 1], rs_recv.at[3 * n + r - 1],
                device_id=along(axis, r), device_id_type=MESH,
            )
            c.start()
            group.append(c)
            copies.append(c)
        return group

    def landed(group):
        for c in group:
            c.wait_recv()

    def rows_a(zz, hh, xx, ll):
        return cf[zz, hh, xx, ll, 0:48, :]

    def pack_a(n, c):
        zz, hh, xx = n // 8, (n // 4) % 2, n % 4
        for ll in range(2):
            s1a[xx, 2 * hh + ll, zz] = rows_a(zz, hh, xx, ll).astype(BF16)
        return c

    l8 = lane((8, 128)) // 16

    def rows_bc(zz, hh, xx):
        mixes = [cmix[zz, hh, xx, u] for u in range(9)]
        tails = ([], [])
        for u in range(0, 8, 2):
            a, b = mixes[u], mixes[u + 1]
            tails[0].append(jnp.where(sub8 < 4, a, pltpu.roll(b, 4, 0)))
            tails[1].append(jnp.where(sub8 < 4, pltpu.roll(a, 4, 0), b))
        mm = mass[pl.ds(pl.multiple_of(64 + 8 * xx, 8), 8), :]
        m0 = mass[pl.ds(pl.multiple_of(8 * xx, 8), 8), :]
        m1 = mass[pl.ds(pl.multiple_of(32 + 8 * xx, 8), 8), :]
        for ll, (m8, m4, last) in enumerate(
            ((m0, pltpu.roll(mm, 4, 0), mixes[8]), (m1, mm, pltpu.roll(mixes[8], 4, 0)))
        ):
            v = jnp.where(l8 < 2, pltpu.roll(m8, 4, 0), jnp.where(l8 < 4, m8, m4))
            vh = v.astype(BF16).astype(F32)
            v = jnp.where(l8 % 2 == 0, vh, v - vh)
            tails[ll].append(jnp.where(sub8 < 4, last, v))
        return [
            (
                jnp.concatenate([cf[zz, hh, xx, ll, 48:72, :], tails[ll][0]], axis=0),
                jnp.concatenate(tails[ll][1:], axis=0),
            )
            for ll in range(2)
        ]

    def pack_bc(n, c):
        zz, hh, xx = n // 8, (n // 4) % 2, n % 4
        for ll, (b, c_) in enumerate(rows_bc(zz, hh, xx)):
            s1b[2 * hh + ll, zz, xx] = b.astype(BF16)
            s1c[zz, xx, 2 * hh + ll] = c_.astype(BF16)
        return c

    lax.fori_loop(0, 6, sums, 0, unroll=3)
    lax.fori_loop(0, 32, pack_a, 0)
    g1a = stage(0, 0, s1a, r1a)
    lax.fori_loop(6, 9, sums, 0, unroll=3)
    lax.fori_loop(0, 32, pack_bc, 0)
    g1b = stage(1, 1, s1b, r1b)
    g1c = stage(2, 2, s1c, r1c)

    def keep_a(n, c):
        for ll in range(2):
            own_a[2 * (n % 2) + ll, n // 2] = rows_a(n // 2, n % 2, x, ll)
        return c

    def keep_b(n, c):
        both = rows_bc(n // 4, yh, n % 4)
        own_b[n // 4, n % 4] = jnp.where(yl == 0, both[0][0], both[1][0])
        return c

    def keep_c(n, c):
        for ll, (_, v) in enumerate(rows_bc(z, n // 4, n % 4)):
            own_c[n % 4, 2 * (n // 4) + ll] = v
        return c

    lax.fori_loop(0, 8, keep_a, 0)
    lax.fori_loop(0, 16, keep_b, 0)
    lax.fori_loop(0, 8, keep_c, 0)

    def add_first(own, got, to):
        def step(n, c):
            i, j = n // 4, n % 4
            to[i, j] = own[i, j] + (got[1, i, j].astype(F32) + got[2, i, j].astype(F32)) + got[3, i, j].astype(F32)
            return c

        lax.fori_loop(0, 16, step, 0)

    def add_second(held, got, to, axis):
        for j in range(4):
            to[j] = held[place[axis], j] + (got[1, j] + got[2, j]) + got[3, j]

    def add_third(held, got, axis):
        return held[place[axis]] + (got[1] + got[2]) + got[3]

    landed(g1a)
    add_first(own_a, r1a, s2a)
    g2a = stage(3, 1, s2a, r2a)
    landed(g1b)
    add_first(own_b, r1b, s2b)
    g2b = stage(4, 2, s2b, r2b)
    landed(g1c)
    add_first(own_c, r1c, s2c)
    g2c = stage(5, 0, s2c, r2c)
    landed(g2a)
    add_second(s2a, r2a, s3a, 1)
    g3a = stage(6, 2, s3a, r3a)
    landed(g2b)
    add_second(s2b, r2b, s3b, 2)
    g3b = stage(7, 0, s3b, r3b)
    landed(g2c)
    add_second(s2c, r2c, s3c, 0)
    g3c = stage(8, 1, s3c, r3c)
    landed(g3a)
    part_a = add_third(s3a, r3a, 2)
    landed(g3b)
    part_b = add_third(s3b, r3b, 0)
    landed(g3c)
    part_c = add_third(s3c, r3c, 1)

    v = jnp.concatenate([part_a, part_b, part_c], axis=0)
    pairs = []
    for u in range(9):
        tail = v[72 + 8 * (u // 2) : 80 + 8 * (u // 2)]
        if u % 2:
            tail = pltpu.roll(tail, 4, 0)
        both = jnp.concatenate([v[8 * u : 8 * u + 8], tail], axis=0)
        comps = [both] + [pltpu.roll(both, 128 - 32 * i, 1) for i in range(1, 4)]
        pairs += [(comps[0], comps[1]), (comps[2], comps[3])]
    s = [w * (1.0 / 36.0) for w in inverse36(pairs)]
    block = lane((16, 128)) // 32
    cols = []
    for b in range(0, 36, 4):
        w = s[b]
        for i in range(1, 4):
            w = jnp.where(block == i, pltpu.roll(s[b + i], 32 * i, 1), w)
        cols.append(w)
    high, low = split(jnp.concatenate(cols, axis=1))
    o = dot(jnp.concatenate([high, low], axis=0), perm[...], NT)
    out[...] = (o[:16] + o[16:])[:12]
    m = v[104:112]
    m = m + pltpu.roll(m, 112, 1)
    l128 = lane((8, 128))
    for k in range(12):
        out_mass[k] = jnp.sum(jnp.where((sub8 == 4 + k % 4) & (l128 == 32 * (k // 4)), m, 0.0))
    for c in copies:
        c.wait_send()
    for c in started:
        c.wait_send()


def column_order():
    q, b, c = np.meshgrid(np.arange(8), np.arange(ROT), np.arange(TURN), indexing="ij")
    perm = np.zeros((BAND, BAND), np.float32)
    perm[(q * ANG + b * TURN + c).ravel(), (b * 32 + q * 4 + c).ravel()] = 1
    return perm


def per_device(images, references, class_prior):
    perm = jnp.asarray(column_order(), BF16)
    vmem = pl.BlockSpec(memory_space=pltpu.VMEM)
    hbm = pl.BlockSpec(memory_space=pl.ANY)
    smem = pl.BlockSpec(memory_space=pltpu.SMEM)
    rows = (48, 32, 32)
    return pl.pallas_call(
        kernel,
        out_shape=(jax.ShapeDtypeStruct((12, BAND), F32), jax.ShapeDtypeStruct((12,), F32)),
        in_specs=[smem, hbm, hbm, hbm],
        out_specs=(pl.BlockSpec(memory_space=pltpu.VMEM), smem),
        scratch_shapes=[
            pltpu.VMEM((64, 9216), BF16),
            pltpu.VMEM((BAND, BAND), BF16),
            pltpu.VMEM((12, 16, 9216), BF16),
            pltpu.VMEM((128, BAND), BF16),
            pltpu.VMEM((2, 36, 64, 256), BF16),
            pltpu.VMEM((HALF, 2, 256, 256), BF16),
            pltpu.VMEM((8, 864, 128), BF16),
            pltpu.VMEM((HALF, 2, 96, 256), F32),
            pltpu.VMEM((8, HALF, 2, 8, 128), F32),
            pltpu.VMEM((8, 16, 128), F32),
            pltpu.VMEM((36, 96, 128), F32),
            pltpu.VMEM((2, 2, 8, 128), F32),
            pltpu.VMEM((HALF, 2, 192, 256), BF16),
            pltpu.VMEM((96, 128), F32),
            pltpu.VMEM((4, 2, 4, 2, 72, 128), F32),
            pltpu.VMEM((4, 2, 4, 9, 8, 128), F32),
            *[pltpu.VMEM((4, 4, r, 128), F32) for r in rows],
            *[pltpu.VMEM((4, 4, 4, r, 128), BF16) for r in rows],
            *[pltpu.VMEM((4, 4, 4, r, 128), BF16) for r in rows],
            *[pltpu.VMEM((4, 4, r, 128), F32) for r in rows],
            *[pltpu.VMEM((4, 4, r, 128), F32) for r in rows],
            *[pltpu.VMEM((4, r, 128), F32) for r in rows],
            *[pltpu.VMEM((4, r, 128), F32) for r in rows],
            pltpu.SemaphoreType.DMA((14,)),
            pltpu.SemaphoreType.DMA((14,)),
            pltpu.SemaphoreType.DMA((14,)),
            pltpu.SemaphoreType.DMA((8,)),
            pltpu.SemaphoreType.DMA((8,)),
            pltpu.SemaphoreType.DMA((2,)),
            pltpu.SemaphoreType.DMA((2,)),
            pltpu.SemaphoreType.DMA((27,)),
            pltpu.SemaphoreType.DMA((27,)),
        ],
        compiler_params=pltpu.CompilerParams(
            collective_id=0, has_side_effects=True, vmem_limit_bytes=56 * 1024 * 1024
        ),
        name="em_pass",
    )(class_prior, images, references, perm)


def solution(mesh):
    placed = (P(("img", "ref"), None), P("ref", None), P("ref"))
    return jax.shard_map(
        per_device,
        mesh=mesh,
        in_specs=placed,
        out_specs=(P("ref", "img"), P("ref")),
        check_vma=False,
    )
```

```python
import math
import jax
import jax.numpy as jnp
from jax import lax
from jax.experimental import pallas as pl
from jax.experimental.pallas import tpu as pltpu
from jax.sharding import PartitionSpec as P

ANG = 144
ROT = 36
TURN = 4
BAND = 1152
HALF = ROT // 2
F32 = jnp.float32
BF16 = jnp.bfloat16
MESH = pl.DeviceIdType.MESH

COS9 = [math.cos(2 * math.pi * m / 9) for m in range(9)]
SIN9 = [math.sin(2 * math.pi * m / 9) for m in range(9)]
ROOT3H = math.sqrt(3.0) / 2


def cos_sums(y0, e):
    t = e[0] + e[1] + e[3]
    top = y0 + e[2]
    base = y0 - 0.5 * e[2]
    out = [top + t]
    for f in (1, 2, 4):
        out.append(base + COS9[f % 9] * e[0] + COS9[2 * f % 9] * e[1] + COS9[4 * f % 9] * e[3])
    out.insert(3, top - 0.5 * t)
    return out


def sin_sums(o):
    h = ROOT3H * o[2]
    one = SIN9[1] * o[0] + SIN9[2] * o[1] + h + SIN9[4] * o[3]
    two = SIN9[2] * o[0] + SIN9[4] * o[1] - h - SIN9[1] * o[3]
    three = ROOT3H * (o[0] - o[1] + o[3])
    four = SIN9[4] * o[0] - SIN9[1] * o[1] + h - SIN9[2] * o[3]
    return [one, two, three, four]


def real9(y):
    e = [y[m] + y[9 - m] for m in range(1, 5)]
    o = [y[m] - y[9 - m] for m in range(1, 5)]
    s = sin_sums(o)
    return cos_sums(y[0], e), [None] + [-v for v in s]


def forward36(x):
    y0, y2, y1r, y1i = [], [], [], []
    for b2 in range(9):
        x0, x1, x2, x3 = (x[(9 * b1 + 4 * b2) % 36] for b1 in range(4))
        u0, u1, v0, v1 = x0 + x2, x0 - x2, x1 + x3, x3 - x1
        y0.append(u0 + v0)
        y2.append(u0 - v0)
        y1r.append(u1)
        y1i.append(v1)
    z0r, z0i = real9(y0)
    z2r, z2i = real9(y2)
    ur, ui = real9(y1r)
    vr, vi = real9(y1i)
    z1r, z1i = [None] * 9, [None] * 9
    z1r[0], z1i[0] = ur[0], vr[0]
    for f in range(1, 5):
        z1r[f], z1i[f] = ur[f] - vi[f], ui[f] + vr[f]
        z1r[9 - f], z1i[9 - f] = ur[f] + vi[f], vr[f] - ui[f]

    def at(f):
        f1, f2 = f % 4, f % 9
        if f1 in (0, 2):
            r, i = (z0r, z0i) if f1 == 0 else (z2r, z2i)
            if f2 == 0:
                return r[0], None
            return (r[f2], i[f2]) if f2 <= 4 else (r[9 - f2], -i[9 - f2])
        if f1 == 1:
            return z1r[f2], z1i[f2]
        g = (9 - f2) % 9
        return z1r[g], -z1i[g]

    return [(at(0)[0], at(18)[0])] + [at(f) for f in range(1, HALF)]


def inverse36(pairs):
    def spec(f):
        f %= 36
        if f == 0:
            return pairs[0][0], None
        if f == 18:
            return pairs[0][1], None
        if f < 18:
            return pairs[f]
        r, i = pairs[36 - f]
        return r, -i

    def find(f1, f2):
        return spec(next(f for f in range(36) if f % 4 == f1 and f % 9 == f2))

    def hermitian(f1):
        r0 = find(f1, 0)[0]
        z = [find(f1, f) for f in range(1, 5)]
        c = cos_sums(r0, [2.0 * r for r, _ in z])
        s = sin_sums([2.0 * i for _, i in z])
        y = [None] * 9
        y[0] = c[0]
        for m in range(1, 5):
            y[m], y[9 - m] = c[m] - s[m - 1], c[m] + s[m - 1]
        return y

    y0, y2 = hermitian(0), hermitian(2)
    z = [find(1, f) for f in range(9)]
    er = [z[f][0] + z[9 - f][0] for f in range(1, 5)]
    ei = [z[f][1] + z[9 - f][1] for f in range(1, 5)]
    dr = [z[f][0] - z[9 - f][0] for f in range(1, 5)]
    di = [z[f][1] - z[9 - f][1] for f in range(1, 5)]
    cr, ci = cos_sums(z[0][0], er), cos_sums(z[0][1], ei)
    sr, si = sin_sums(dr), sin_sums(di)
    y1r, y1i = [cr[0]] + [None] * 8, [ci[0]] + [None] * 8
    for m in range(1, 5):
        y1r[m], y1r[9 - m] = cr[m] - si[m - 1], cr[m] + si[m - 1]
        y1i[m], y1i[9 - m] = ci[m] + sr[m - 1], ci[m] - sr[m - 1]
    x = [None] * 36
    for b2 in range(9):
        p, q = y0[b2] + y2[b2], y0[b2] - y2[b2]
        a, b = 2.0 * y1r[b2], 2.0 * y1i[b2]
        for b1, v in enumerate((p + a, q - b, p - a, q + b)):
            x[(9 * b1 + 4 * b2) % 36] = v
    return x


def lane(shape):
    return lax.broadcasted_iota(jnp.int32, shape, len(shape) - 1)


def turn32(a):
    l = lane(a[0].shape)
    low = l < 64
    even = (l // 32) % 2 == 0
    b0 = jnp.where(low, a[0], pltpu.roll(a[2], 64, 1))
    b2 = jnp.where(low, pltpu.roll(a[0], 64, 1), a[2])
    b1 = jnp.where(low, a[1], pltpu.roll(a[3], 64, 1))
    b3 = jnp.where(low, pltpu.roll(a[1], 64, 1), a[3])
    out = []
    for p, q in ((b0, b1), (b2, b3)):
        out.append(jnp.where(even, p, pltpu.roll(q, 32, 1)))
        out.append(jnp.where(even, pltpu.roll(p, 96, 1), q))
    return out


def split(v):
    h = v.astype(BF16)
    return h, (v - h.astype(F32)).astype(BF16)


NT = (((1,), (1,)), ((), ()))
NN = (((1,), (0,)), ((), ()))


def dot(a, b, dims=NN):
    return lax.dot_general(a, b, dims, preferred_element_type=F32)


def kernel(
    prior_hbm, images_hbm, refs, out, out_mass,
    prior, images, perm, rows16, tload, x5, xh, tbuf, tf, tmix, offs, sh, stat, lh, mass, cf, cmix,
    own_a, own_b, own_c, s1a, s1b, s1c, r1a, r1b, r1c, s2a, s2b, s2c, r2a, r2b, r2c, s3a, s3b, s3c, r3a, r3b, r3c,
    load_sem, send_sem, recv_sem, off_send, off_recv, pair_send, pair_recv, rs_send, rs_recv,
):
    img, ref = lax.axis_index("img"), lax.axis_index("ref")
    z, yh = img // 2, img % 2
    x, yl, core = ref // 4, (ref // 2) % 2, ref % 2

    def dev(x_, y_, z_, c_):
        return {"img": z_ * 2 + y_ // 2, "ref": x_ * 4 + (y_ % 2) * 2 + c_}

    y = yh * 2 + yl
    xp, xm = (x + 1) % 4, (x + 3) % 4
    x2 = (x + 2) % 4
    to_xp, to_xm = dev(xp, y, z, core), dev(xm, y, z, core)
    to_yp, to_ym = dev(x, (y + 1) % 4, z, core), dev(x, (y + 3) % 4, z, core)
    sibling = dev(x, y, z, 1 - core)

    loads = []
    for k in range(12):
        c = pltpu.make_async_copy(refs.at[pl.ds(36 * k // 16 * 16, 16)], rows16.at[k], load_sem.at[k])
        c.start()
        loads.append(c)
    load_prior = pltpu.make_async_copy(prior_hbm, prior, load_sem.at[12])
    load_prior.start()
    load_images = pltpu.make_async_copy(images_hbm, images, load_sem.at[13])
    load_images.start()

    def along(axis, r):
        x_, y_, z_ = ((v + r * (a == axis)) % 4 for a, v in enumerate((x, y, z)))
        return dev(x_, y_, z_, core)

    def away(d):
        return dev((x + d // 2) % 4, yh * 2 + (yl + d) % 2, z, core)

    barrier = pltpu.get_barrier_semaphore()
    partners = [along(a, r) for a in range(3) for r in range(1, 4)] + [away(d) for d in (3, 5, 7)] + [sibling]
    for p in partners:
        pl.semaphore_signal(barrier, inc=1, device_id=p, device_id_type=MESH)
    def permutation(n, c):
        i = n * 128 + lax.broadcasted_iota(jnp.int32, (128, 128), 0)
        cycle = jnp.zeros_like(i)
        for q in range(1, 8):
            cycle = cycle + jnp.where(i >= ANG * q, 1, 0)
        i = i - ANG * cycle
        to = (i >> 2) * 32 + cycle * 4 + (i & 3) - lane((128, 128))
        for v in range(9):
            perm[pl.ds(pl.multiple_of(n * 128, 128), 128), v * 128 : v * 128 + 128] = jnp.where(
                to == 128 * v, 1.0, 0.0
            ).astype(BF16)
        return c

    lax.fori_loop(0, 9, permutation, 0)

    for c in loads:
        c.wait()
    norm = jnp.zeros((16, 128), F32)
    for g in range(8):
        tiles = []
        for k in range(12):
            at = 36 * k % 16
            tiles.append(rows16[k, :, g * BAND : (g + 1) * BAND].astype(F32)[at : at + 1])
        tiles.append(jnp.zeros((4, BAND), F32))
        t = jnp.concatenate(tiles, axis=0)
        for v in range(9):
            part = t[:, v * 128 : (v + 1) * 128]
            norm = norm + part * part
        tload[g * 16 : (g + 1) * 16, :] = t.astype(BF16)
    half_norm = 0.5 * jnp.sum(norm, axis=1, keepdims=True)
    rowid = lax.broadcasted_iota(jnp.int32, (16, 128), 0)
    load_prior.wait()
    pri = jnp.ones((16, 128), F32)
    for k in range(12):
        pri = jnp.where(rowid == k, prior[k], pri)
    slot = x * 2 + yl
    offs[slot] = jnp.log(pri) - half_norm

    sub8 = lax.broadcasted_iota(jnp.int32, (8, 128), 0)

    def arrange(v, c):
        o = dot(tload[...], perm[:, pl.ds(pl.multiple_of(v * 128, 128), 128)])
        halves = [turn32([o[(2 * zz + h) * 16 : (2 * zz + h) * 16 + 16] for zz in range(4)]) for h in range(2)]
        rows = []
        for i in range(4):
            a, b = halves[0][i], halves[1][i]
            rows += [a[:8], b[:8], jnp.where(sub8 < 4, a[8:], pltpu.roll(b[8:], 4, 0))]
        tbuf[slot, pl.ds(pl.multiple_of(96 * v, 32), 96), :] = jnp.concatenate(rows, axis=0).astype(BF16)
        return c

    lax.fori_loop(0, 9, arrange, 0, unroll=9)

    pl.semaphore_wait(barrier, len(partners))

    PIECES = ((0, 224), (224, 208), (432, 224), (656, 208))

    def piece(s, p):
        return tbuf.at[s, pl.ds(*PIECES[p])]

    started = []

    def send(s, p, target, n):
        c = pltpu.make_async_remote_copy(
            piece(s, p), piece(s, p), send_sem.at[n], recv_sem.at[n], device_id=target, device_id_type=MESH
        )
        c.start()
        started.append(c)

    def arrived(s, p, n):
        pltpu.make_async_copy(piece(s, p), piece(s, p), recv_sem.at[n]).wait()

    for k in range(2):
        send(slot, k, to_xp, k)
        send(slot, 2 + k, to_xm, 6 + k)
        send(slot, k, to_yp, 12 + k)
        send(slot, 2 + k, to_ym, 14 + k)
    for k in range(2):
        send(slot, 2 + k, to_xp, 2 + k)
        send(slot, k, to_xm, 4 + k)
    off_copies = []
    for d in range(1, 8):
        c = pltpu.make_async_remote_copy(
            offs.at[slot], offs.at[slot], off_send.at[d], off_recv.at[d], device_id=away(d), device_id_type=MESH
        )
        c.start()
        off_copies.append(c)
    s_m, s_p, s_2 = xm * 2 + yl, xp * 2 + yl, x2 * 2 + yl
    o_0, o_m, o_p, o_2 = x * 2 + 1 - yl, xm * 2 + 1 - yl, xp * 2 + 1 - yl, x2 * 2 + 1 - yl

    load_images.wait()
    for g in range(3):
        cols = slice(g * 384, g * 384 + 384)
        stacked = jnp.concatenate([images[:, q * BAND : (q + 1) * BAND] for q in range(8)], axis=0)
        o = dot(stacked, perm[:, cols])
        parts = [o[q * 64 : q * 64 + 64] for q in range(8)]
        for vv in range(3):
            v = 3 * g + vv
            for h in range(2):
                t = turn32([parts[2 * zz + h][:, vv * 128 : vv * 128 + 128] for zz in range(4)])
                for i in range(4):
                    x5[core, 4 * v + i, :, h * 128 : h * 128 + 128] = t[i].astype(BF16)
    swap = pltpu.make_async_remote_copy(
        x5.at[core], x5.at[core], pair_send.at[0], pair_recv.at[0], device_id=sibling, device_id_type=MESH
    )
    swap.start()

    for k in range(2):
        arrived(s_m, k, k)
        send(s_m, k, to_xp, 8 + k)
        send(s_m, k, to_yp, 16 + k)
        arrived(s_p, 2 + k, 6 + k)
        send(s_p, 2 + k, to_xm, 10 + k)
        send(s_p, 2 + k, to_ym, 22 + k)

    def image_spectra(c):
        def step(n, carry):
            t, h = n // 2, n % 2
            r0 = pl.multiple_of(t * 16, 16)
            lanes = pl.ds(pl.multiple_of(h * 128, 128), 128)
            p = forward36([x5[c, b, pl.ds(r0, 16), lanes].astype(F32) for b in range(36)])
            for f in range(HALF):
                for ri in range(2):
                    a, b = split(p[f][ri])
                    at = pl.ds(pl.multiple_of(ri * 128 + c * 64 + r0, 16), 16)
                    xh[f, 0, at, lanes] = a
                    xh[f, 1, at, lanes] = b
            return carry

        lax.fori_loop(0, 8, step, 0)

    image_spectra(core)
    for k in range(2):
        arrived(s_p, k, 4 + k)
        send(s_p, k, to_yp, 20 + k)
        arrived(s_m, 2 + k, 2 + k)
        send(s_m, 2 + k, to_ym, 18 + k)
    swap.wait()
    image_spectra(1 - core)
    for k in range(2):
        arrived(s_2, k, 8 + k)
        send(s_2, k, to_yp, 24 + k)
        arrived(s_2, 2 + k, 10 + k)
        send(s_2, 2 + k, to_ym, 26 + k)

    def distance(i):
        return jnp.where(i == 3, 2, jnp.where(i == 2, 3, i))

    def row(i, part):
        return jnp.where(i == 3, 72 + 8 * part, 24 * part + 8 * i)

    def template_spectra(i, ll):
        s = (x + distance(i)) % 4 * 2 + ll
        raw = []
        for b in range(HALF):
            two = tbuf[s, 48 * b : 48 * b + 48, :].astype(F32)
            raw += [two[:24], two[24:]]
        p = forward36(raw)
        at = pl.ds(pl.multiple_of(row(i, ll), 8), 8)
        for f in range(HALF):
            for ri in range(2):
                v = p[f][ri]
                tf[f, ri, at, 0:128] = v[0:8]
                tf[f, ri, at, 128:256] = v[8:16]
                tmix[i, ll, f, ri] = v[16:24]

    def score_part(members, lo, hi):
        count = hi - lo

        def score(f, c):
            for ri in range(2):
                for i in members:
                    a, b = tmix[i, 0, f, ri], tmix[i, 1, f, ri]
                    at = 88 if i == 3 else 48 + 8 * i
                    tf[f, ri, at : at + 8, 0:128] = jnp.where(sub8 < 4, a, pltpu.roll(b, 4, 0))
                    tf[f, ri, at : at + 8, 128:256] = jnp.where(sub8 < 4, pltpu.roll(a, 4, 0), b)
            high, low = split(jnp.concatenate([tf[f, 0, lo:hi, :], tf[f, 1, lo:hi, :]], axis=0))
            m = dot(high, xh[f, 0], NT) + (dot(low, xh[f, 0], NT) + dot(high, xh[f, 1], NT))
            rr, ri_, ir, ii = m[:count, :128], m[:count, 128:], m[count:, :128], m[count:, 128:]
            first = f == 0
            sh[2 * f, lo:hi, :] = jnp.where(first, rr, rr + ii)
            sh[2 * f + 1, lo:hi, :] = jnp.where(first, ii, ri_ - ir)
            return c

        lax.fori_loop(0, HALF, score, 0, unroll=6)

    def own_row(i, c):
        template_spectra(i, yl)
        return c

    def other_row(i, c):
        template_spectra(i, 1 - yl)
        return c

    lax.fori_loop(0, 4, own_row, 0)
    for p in range(4):
        arrived(o_0, p, 12 + p)
    for p in range(4):
        arrived(o_m, p, 16 + p)
        arrived(o_p, p, 20 + p)
    lax.fori_loop(0, 3, other_row, 0)
    score_part((0, 1, 2), 0, 72)
    for p in range(4):
        arrived(o_2, p, 24 + p)
    lax.fori_loop(3, 4, other_row, 0)
    score_part((3,), 72, 96)
    for c in off_copies:
        c.wait()

    def to_turns(off, rows, top):
        p = [(sh[2 * f, rows, :], sh[2 * f + 1, rows, :]) for f in range(HALF)]
        s = inverse36(p)
        for r in range(36):
            v = s[r] * (1.0 / 36.0) + off
            sh[r, rows, :] = v
            top = jnp.maximum(top, v)
        return top

    def rows_of(n, c):
        i = jnp.where(n < 9, n % 3, 3)
        part = jnp.where(n < 9, n // 3, n - 9)
        at = (x + distance(i)) % 4 * 2
        a, b = offs[at], offs[at + 1]
        last = jnp.where(sub8 < 4, a[8:], pltpu.roll(b[8:], 4, 0))
        off = jnp.where(part == 0, a[:8], jnp.where(part == 1, b[:8], last))
        return to_turns(off, pl.ds(pl.multiple_of(n * 8, 8), 8), c)

    top8 = lax.fori_loop(0, 12, rows_of, jnp.full((8, 128), -jnp.inf, F32))
    top = jnp.max(top8, axis=0, keepdims=True)

    def raise_(n, c):
        rows = pl.ds(pl.multiple_of(n * 8, 8), 8)
        for r in range(36):
            e = jnp.exp(sh[r, rows, :] - top)
            sh[r, rows, :] = e
            c = c + e
        return c

    total = jnp.sum(lax.fori_loop(0, 12, raise_, jnp.zeros((8, 128), F32)), axis=0, keepdims=True)
    stat[0, 0] = jnp.broadcast_to(top, (8, 128))
    stat[0, 1] = jnp.broadcast_to(total, (8, 128))
    share = pltpu.make_async_remote_copy(
        stat.at[0], stat.at[1], pair_send.at[1], pair_recv.at[1], device_id=sibling, device_id_type=MESH
    )
    share.start()
    share.wait()
    top_o, total_o = stat[1, 0][:1], stat[1, 1][:1]
    peak = jnp.maximum(top, top_o)
    mine = jnp.exp(top - peak)
    scale = mine / (total * mine + total_o * jnp.exp(top_o - peak))

    def weigh(n, c):
        rows = pl.ds(pl.multiple_of(n * 16, 16), 16)
        upper = pl.ds(pl.multiple_of(n * 16 + 96, 16), 16)
        w = [(sh[r, rows, :] * scale).astype(BF16).astype(F32) for r in range(36)]
        p = forward36(w)
        mass[rows, :] = jnp.broadcast_to(jnp.sum(p[0][0], axis=1, keepdims=True), (16, 128))
        none = jnp.zeros((16, 128), BF16)
        for f in range(HALF):
            for part, (r, i) in enumerate(zip(split(p[f][0]), split(p[f][1]))):
                lh[f, part, rows, 0:128] = r
                lh[f, part, rows, 128:256] = none if f == 0 else i
                lh[f, part, upper, 0:128] = none if f == 0 else -i
                lh[f, part, upper, 128:256] = i if f == 0 else r
        return c

    lax.fori_loop(0, 6, weigh, 0)

    def sums(u, c):
        comps = []
        for ff in range(2):
            f = 2 * u + ff
            a, b = lh[f, 0], lh[f, 1]
            m = dot(a, xh[f, 0]) + (dot(b, xh[f, 0]) + dot(a, xh[f, 1]))
            comps += [m[:96], m[96:]]
        at = pl.ds(pl.multiple_of(8 * u, 8), 8)
        for h in range(2):
            t = turn32([v[:, h * 128 : h * 128 + 128] for v in comps])
            for zz in range(4):
                for i in range(4):
                    xx = (x + (0, 1, 3, 2)[i]) % 4
                    r = [72 + 8 * p if i == 3 else 24 * p + 8 * i for p in range(3)]
                    cf[zz, h, xx, 0, at, :] = t[zz][r[0] : r[0] + 8]
                    cf[zz, h, xx, 1, at, :] = t[zz][r[1] : r[1] + 8]
                    cmix[zz, h, xx, u] = t[zz][r[2] : r[2] + 8]
        return c

    place = (x, y, z)
    copies = []

    ORDER = (2, 1, 3, 0)

    def go(n, axis, r, src, dst):
        c = pltpu.make_async_remote_copy(
            src, dst, rs_send.at[n], rs_recv.at[n], device_id=along(axis, r), device_id_type=MESH
        )
        c.start()
        copies.append(c)
        return c

    def first_stage(share, axis, second, src, dst):
        groups = {}
        for k in ORDER:
            to = (place[second] + k) % 4
            groups[k] = [
                go(12 * share + 3 * k + r - 1, axis, r, src.at[(place[axis] + r) % 4, to], dst.at[r, to])
                for r in range(1, 4)
            ]
        return groups

    def landed(group):
        for c in group:
            c.wait_recv()

    def rows_a(zz, hh, xx, ll):
        return cf[zz, hh, xx, ll, 0:48, :]

    def pack_a(n, c):
        zz, hh, xx = n // 8, (n // 4) % 2, n % 4
        for ll in range(2):
            s1a[xx, 2 * hh + ll, zz] = rows_a(zz, hh, xx, ll).astype(BF16)
        return c

    l8 = lane((8, 128)) // 16

    def rows_bc(zz, hh, xx):
        mixes = [cmix[zz, hh, xx, u] for u in range(9)]
        tails = ([], [])
        for u in range(0, 8, 2):
            a, b = mixes[u], mixes[u + 1]
            tails[0].append(jnp.where(sub8 < 4, a, pltpu.roll(b, 4, 0)))
            tails[1].append(jnp.where(sub8 < 4, pltpu.roll(a, 4, 0), b))
        d = (xx - x + 4) % 4
        i = distance(d)
        m0, m1, mm = (mass[pl.ds(pl.multiple_of(row(i, p), 8), 8), :] for p in range(3))
        for ll, (m8, m4, last) in enumerate(
            ((m0, pltpu.roll(mm, 4, 0), mixes[8]), (m1, mm, pltpu.roll(mixes[8], 4, 0)))
        ):
            v = jnp.where(l8 < 2, pltpu.roll(m8, 4, 0), jnp.where(l8 < 4, m8, m4))
            vh = v.astype(BF16).astype(F32)
            v = jnp.where(l8 % 2 == 0, vh, v - vh)
            tails[ll].append(jnp.where(sub8 < 4, last, v))
        return [
            (
                jnp.concatenate([cf[zz, hh, xx, ll, 48:72, :], tails[ll][0]], axis=0),
                jnp.concatenate(tails[ll][1:], axis=0),
            )
            for ll in range(2)
        ]

    def pack_bc(n, c):
        zz, hh, xx = n // 8, (n // 4) % 2, n % 4
        for ll, (b, c_) in enumerate(rows_bc(zz, hh, xx)):
            s1b[2 * hh + ll, zz, xx] = b.astype(BF16)
            s1c[zz, xx, 2 * hh + ll] = c_.astype(BF16)
        return c

    lax.fori_loop(0, 6, sums, 0, unroll=3)
    lax.fori_loop(0, 32, pack_a, 0)
    g1a = first_stage(0, 0, 1, s1a, r1a)
    lax.fori_loop(6, 9, sums, 0, unroll=3)
    lax.fori_loop(0, 32, pack_bc, 0)
    g1b = first_stage(1, 1, 2, s1b, r1b)
    g1c = first_stage(2, 2, 0, s1c, r1c)

    def keep_a(n, c):
        for ll in range(2):
            own_a[2 * (n % 2) + ll, n // 2] = rows_a(n // 2, n % 2, x, ll)
        return c

    def keep_b(n, c):
        both = rows_bc(n // 4, yh, n % 4)
        own_b[n // 4, n % 4] = jnp.where(yl == 0, both[0][0], both[1][0])
        return c

    def keep_c(n, c):
        for ll, (_, v) in enumerate(rows_bc(z, n // 4, n % 4)):
            own_c[n % 4, 2 * (n // 4) + ll] = v
        return c

    lax.fori_loop(0, 8, keep_a, 0)
    lax.fori_loop(0, 16, keep_b, 0)
    lax.fori_loop(0, 8, keep_c, 0)

    shares = (
        (g1a, own_a, r1a, s2a, r2a, s3a, r3a, 1, 2),
        (g1b, own_b, r1b, s2b, r2b, s3b, r3b, 2, 0),
        (g1c, own_c, r1c, s2c, r2c, s3c, r3c, 0, 1),
    )
    g2 = ([], [], [])
    for k in ORDER:
        for share, (g1, own, r1, s2, r2, s3, r3, second, third) in enumerate(shares):
            landed(g1[k])
            to = (place[second] + k) % 4
            for j in range(4):
                s2[to, j] = own[to, j] + (r1[1, to, j].astype(F32) + r1[2, to, j].astype(F32)) + r1[3, to, j].astype(F32)
            if k:
                g2[share].append(go(36 + 3 * share + k - 1, second, k, s2.at[to], r2.at[k]))
    g3 = []
    for share, (g1, own, r1, s2, r2, s3, r3, second, third) in enumerate(shares):
        landed(g2[share])
        for j in range(4):
            s3[j] = s2[place[second], j] + (r2[1, j] + r2[2, j]) + r2[3, j]
        g3.append(
            [
                go(45 + 3 * share + k - 1, third, k, s3.at[(place[third] + k) % 4], r3.at[k])
                for k in range(1, 4)
            ]
        )

    def add_third(held, got, axis):
        return held[place[axis]] + (got[1] + got[2]) + got[3]

    g3a, g3b, g3c = g3
    landed(g3a)
    part_a = add_third(s3a, r3a, 2)
    landed(g3b)
    part_b = add_third(s3b, r3b, 0)
    landed(g3c)
    part_c = add_third(s3c, r3c, 1)

    v = jnp.concatenate([part_a, part_b, part_c], axis=0)
    pairs = []
    for u in range(9):
        tail = v[72 + 8 * (u // 2) : 80 + 8 * (u // 2)]
        if u % 2:
            tail = pltpu.roll(tail, 4, 0)
        both = jnp.concatenate([v[8 * u : 8 * u + 8], tail], axis=0)
        comps = [both] + [pltpu.roll(both, 128 - 32 * i, 1) for i in range(1, 4)]
        pairs += [(comps[0], comps[1]), (comps[2], comps[3])]
    s = [w * (1.0 / 36.0) for w in inverse36(pairs)]
    block = lane((16, 128)) // 32
    cols = []
    for b in range(0, 36, 4):
        w = s[b]
        for i in range(1, 4):
            w = jnp.where(block == i, pltpu.roll(s[b + i], 32 * i, 1), w)
        cols.append(w)
    high, low = split(jnp.concatenate(cols, axis=1))
    o = dot(jnp.concatenate([high, low], axis=0), perm[...], NT)
    out[...] = (o[:16] + o[16:])[:12]
    m = v[104:112]
    m = m + pltpu.roll(m, 112, 1)
    l128 = lane((8, 128))
    for k in range(12):
        out_mass[k] = jnp.sum(jnp.where((sub8 == 4 + k % 4) & (l128 == 32 * (k // 4)), m, 0.0))
    for c in copies:
        c.wait_send()
    for c in started:
        c.wait_send()


def per_device(images, references, class_prior):
    hbm = pl.BlockSpec(memory_space=pl.ANY)
    smem = pl.BlockSpec(memory_space=pltpu.SMEM)
    rows = (48, 32, 32)
    return pl.pallas_call(
        kernel,
        out_shape=(jax.ShapeDtypeStruct((12, BAND), F32), jax.ShapeDtypeStruct((12,), F32)),
        in_specs=[hbm, hbm, hbm],
        out_specs=(pl.BlockSpec(memory_space=pltpu.VMEM), smem),
        scratch_shapes=[
            pltpu.SMEM((12,), F32),
            pltpu.VMEM((64, 9216), BF16),
            pltpu.VMEM((BAND, BAND), BF16),
            pltpu.VMEM((12, 16, 9216), BF16),
            pltpu.VMEM((128, BAND), BF16),
            pltpu.VMEM((2, 36, 64, 256), BF16),
            pltpu.VMEM((HALF, 2, 256, 256), BF16),
            pltpu.VMEM((8, 864, 128), BF16),
            pltpu.VMEM((HALF, 2, 96, 256), F32),
            pltpu.VMEM((4, 2, HALF, 2, 8, 128), F32),
            pltpu.VMEM((8, 16, 128), F32),
            pltpu.VMEM((36, 96, 128), F32),
            pltpu.VMEM((2, 2, 8, 128), F32),
            pltpu.VMEM((HALF, 2, 192, 256), BF16),
            pltpu.VMEM((96, 128), F32),
            pltpu.VMEM((4, 2, 4, 2, 72, 128), F32),
            pltpu.VMEM((4, 2, 4, 9, 8, 128), F32),
            *[pltpu.VMEM((4, 4, r, 128), F32) for r in rows],
            *[pltpu.VMEM((4, 4, 4, r, 128), BF16) for r in rows],
            *[pltpu.VMEM((4, 4, 4, r, 128), BF16) for r in rows],
            *[pltpu.VMEM((4, 4, r, 128), F32) for r in rows],
            *[pltpu.VMEM((4, 4, r, 128), F32) for r in rows],
            *[pltpu.VMEM((4, r, 128), F32) for r in rows],
            *[pltpu.VMEM((4, r, 128), F32) for r in rows],
            pltpu.SemaphoreType.DMA((14,)),
            pltpu.SemaphoreType.DMA((28,)),
            pltpu.SemaphoreType.DMA((28,)),
            pltpu.SemaphoreType.DMA((8,)),
            pltpu.SemaphoreType.DMA((8,)),
            pltpu.SemaphoreType.DMA((2,)),
            pltpu.SemaphoreType.DMA((2,)),
            pltpu.SemaphoreType.DMA((54,)),
            pltpu.SemaphoreType.DMA((54,)),
        ],
        compiler_params=pltpu.CompilerParams(
            collective_id=0, has_side_effects=True, vmem_limit_bytes=56 * 1024 * 1024
        ),
        name="em_pass",
    )(class_prior, images, references)


def solution(mesh):
    placed = (P(("img", "ref"), None), P("ref", None), P("ref"))
    return jax.shard_map(
        per_device,
        mesh=mesh,
        in_specs=placed,
        out_specs=(P("ref", "img"), P("ref")),
        check_vma=False,
    )
```

```python
import math
import jax
import jax.numpy as jnp
from jax import lax
from jax.experimental import pallas as pl
from jax.experimental.pallas import tpu as pltpu
from jax.sharding import PartitionSpec as P

ANG = 144
ROT = 36
TURN = 4
BAND = 1152
HALF = ROT // 2
F32 = jnp.float32
BF16 = jnp.bfloat16
MESH = pl.DeviceIdType.MESH

COS9 = [math.cos(2 * math.pi * m / 9) for m in range(9)]
SIN9 = [math.sin(2 * math.pi * m / 9) for m in range(9)]
ROOT3H = math.sqrt(3.0) / 2


def cos_sums(y0, e):
    t = e[0] + e[1] + e[3]
    top = y0 + e[2]
    base = y0 - 0.5 * e[2]
    out = [top + t]
    for f in (1, 2, 4):
        out.append(base + COS9[f % 9] * e[0] + COS9[2 * f % 9] * e[1] + COS9[4 * f % 9] * e[3])
    out.insert(3, top - 0.5 * t)
    return out


def sin_sums(o):
    h = ROOT3H * o[2]
    one = SIN9[1] * o[0] + SIN9[2] * o[1] + h + SIN9[4] * o[3]
    two = SIN9[2] * o[0] + SIN9[4] * o[1] - h - SIN9[1] * o[3]
    three = ROOT3H * (o[0] - o[1] + o[3])
    four = SIN9[4] * o[0] - SIN9[1] * o[1] + h - SIN9[2] * o[3]
    return [one, two, three, four]


def real9(y):
    e = [y[m] + y[9 - m] for m in range(1, 5)]
    o = [y[m] - y[9 - m] for m in range(1, 5)]
    s = sin_sums(o)
    return cos_sums(y[0], e), [None] + [-v for v in s]


def forward36(x):
    y0, y2, y1r, y1i = [], [], [], []
    for b2 in range(9):
        x0, x1, x2, x3 = (x[(9 * b1 + 4 * b2) % 36] for b1 in range(4))
        u0, u1, v0, v1 = x0 + x2, x0 - x2, x1 + x3, x3 - x1
        y0.append(u0 + v0)
        y2.append(u0 - v0)
        y1r.append(u1)
        y1i.append(v1)
    z0r, z0i = real9(y0)
    z2r, z2i = real9(y2)
    ur, ui = real9(y1r)
    vr, vi = real9(y1i)
    z1r, z1i = [None] * 9, [None] * 9
    z1r[0], z1i[0] = ur[0], vr[0]
    for f in range(1, 5):
        z1r[f], z1i[f] = ur[f] - vi[f], ui[f] + vr[f]
        z1r[9 - f], z1i[9 - f] = ur[f] + vi[f], vr[f] - ui[f]

    def at(f):
        f1, f2 = f % 4, f % 9
        if f1 in (0, 2):
            r, i = (z0r, z0i) if f1 == 0 else (z2r, z2i)
            if f2 == 0:
                return r[0], None
            return (r[f2], i[f2]) if f2 <= 4 else (r[9 - f2], -i[9 - f2])
        if f1 == 1:
            return z1r[f2], z1i[f2]
        g = (9 - f2) % 9
        return z1r[g], -z1i[g]

    return [(at(0)[0], at(18)[0])] + [at(f) for f in range(1, HALF)]


def inverse36(pairs):
    def spec(f):
        f %= 36
        if f == 0:
            return pairs[0][0], None
        if f == 18:
            return pairs[0][1], None
        if f < 18:
            return pairs[f]
        r, i = pairs[36 - f]
        return r, -i

    def find(f1, f2):
        return spec(next(f for f in range(36) if f % 4 == f1 and f % 9 == f2))

    def hermitian(f1):
        r0 = find(f1, 0)[0]
        z = [find(f1, f) for f in range(1, 5)]
        c = cos_sums(r0, [2.0 * r for r, _ in z])
        s = sin_sums([2.0 * i for _, i in z])
        y = [None] * 9
        y[0] = c[0]
        for m in range(1, 5):
            y[m], y[9 - m] = c[m] - s[m - 1], c[m] + s[m - 1]
        return y

    y0, y2 = hermitian(0), hermitian(2)
    z = [find(1, f) for f in range(9)]
    er = [z[f][0] + z[9 - f][0] for f in range(1, 5)]
    ei = [z[f][1] + z[9 - f][1] for f in range(1, 5)]
    dr = [z[f][0] - z[9 - f][0] for f in range(1, 5)]
    di = [z[f][1] - z[9 - f][1] for f in range(1, 5)]
    cr, ci = cos_sums(z[0][0], er), cos_sums(z[0][1], ei)
    sr, si = sin_sums(dr), sin_sums(di)
    y1r, y1i = [cr[0]] + [None] * 8, [ci[0]] + [None] * 8
    for m in range(1, 5):
        y1r[m], y1r[9 - m] = cr[m] - si[m - 1], cr[m] + si[m - 1]
        y1i[m], y1i[9 - m] = ci[m] + sr[m - 1], ci[m] - sr[m - 1]
    x = [None] * 36
    for b2 in range(9):
        p, q = y0[b2] + y2[b2], y0[b2] - y2[b2]
        a, b = 2.0 * y1r[b2], 2.0 * y1i[b2]
        for b1, v in enumerate((p + a, q - b, p - a, q + b)):
            x[(9 * b1 + 4 * b2) % 36] = v
    return x


def lane(shape):
    return lax.broadcasted_iota(jnp.int32, shape, len(shape) - 1)


def turn32(a):
    l = lane(a[0].shape)
    low = l < 64
    even = (l // 32) % 2 == 0
    b0 = jnp.where(low, a[0], pltpu.roll(a[2], 64, 1))
    b2 = jnp.where(low, pltpu.roll(a[0], 64, 1), a[2])
    b1 = jnp.where(low, a[1], pltpu.roll(a[3], 64, 1))
    b3 = jnp.where(low, pltpu.roll(a[1], 64, 1), a[3])
    out = []
    for p, q in ((b0, b1), (b2, b3)):
        out.append(jnp.where(even, p, pltpu.roll(q, 32, 1)))
        out.append(jnp.where(even, pltpu.roll(p, 96, 1), q))
    return out


def split(v):
    h = v.astype(BF16)
    return h, (v - h.astype(F32)).astype(BF16)


NT = (((1,), (1,)), ((), ()))
NN = (((1,), (0,)), ((), ()))


def dot(a, b, dims=NN):
    return lax.dot_general(a, b, dims, preferred_element_type=F32)


def kernel(
    prior_hbm, images_hbm, refs, out, out_mass,
    prior, images, perm, rows16, tload, x5, xh, tbuf, tf, tmix, offs, sh, stat, lh, mass, cf, cmix,
    own_a, own_b, own_c, s1a, s1b, s1c, r1a, r1b, r1c, s2a, s2b, s2c, r2a, r2b, r2c, s3a, s3b, s3c, r3a, r3b, r3c,
    load_sem, send_sem, recv_sem, off_send, off_recv, pair_send, pair_recv, rs_send, rs_recv,
):
    img, ref = lax.axis_index("img"), lax.axis_index("ref")
    z, yh = img // 2, img % 2
    x, yl, core = ref // 4, (ref // 2) % 2, ref % 2

    def dev(x_, y_, z_, c_):
        return {"img": z_ * 2 + y_ // 2, "ref": x_ * 4 + (y_ % 2) * 2 + c_}

    y = yh * 2 + yl
    xp, xm = (x + 1) % 4, (x + 3) % 4
    x2 = (x + 2) % 4
    to_xp, to_xm = dev(xp, y, z, core), dev(xm, y, z, core)
    to_yp, to_ym = dev(x, (y + 1) % 4, z, core), dev(x, (y + 3) % 4, z, core)
    sibling = dev(x, y, z, 1 - core)

    loads = []
    for k in range(12):
        c = pltpu.make_async_copy(refs.at[pl.ds(36 * k // 16 * 16, 16)], rows16.at[k], load_sem.at[k])
        c.start()
        loads.append(c)
    load_prior = pltpu.make_async_copy(prior_hbm, prior, load_sem.at[12])
    load_prior.start()
    load_images = pltpu.make_async_copy(images_hbm, images, load_sem.at[13])
    load_images.start()

    def along(axis, r):
        x_, y_, z_ = ((v + r * (a == axis)) % 4 for a, v in enumerate((x, y, z)))
        return dev(x_, y_, z_, core)

    def away(d):
        return dev((x + d // 2) % 4, yh * 2 + (yl + d) % 2, z, core)

    barrier = pltpu.get_barrier_semaphore()
    partners = [along(a, r) for a in range(3) for r in range(1, 4)] + [away(d) for d in (3, 5, 7)] + [sibling]
    for p in partners:
        pl.semaphore_signal(barrier, inc=1, device_id=p, device_id_type=MESH)
    def permutation(n, c):
        i = n * 128 + lax.broadcasted_iota(jnp.int32, (128, 128), 0)
        cycle = jnp.zeros_like(i)
        for q in range(1, 8):
            cycle = cycle + jnp.where(i >= ANG * q, 1, 0)
        i = i - ANG * cycle
        to = (i >> 2) * 32 + cycle * 4 + (i & 3) - lane((128, 128))
        for v in range(9):
            perm[pl.ds(pl.multiple_of(n * 128, 128), 128), v * 128 : v * 128 + 128] = jnp.where(
                to == 128 * v, 1.0, 0.0
            ).astype(BF16)
        return c

    lax.fori_loop(0, 9, permutation, 0)

    for c in loads:
        c.wait()
    norm = jnp.zeros((16, 128), F32)
    for g in range(8):
        tiles = []
        for k in range(12):
            at = 36 * k % 16
            tiles.append(rows16[k, :, g * BAND : (g + 1) * BAND].astype(F32)[at : at + 1])
        tiles.append(jnp.zeros((4, BAND), F32))
        t = jnp.concatenate(tiles, axis=0)
        for v in range(9):
            part = t[:, v * 128 : (v + 1) * 128]
            norm = norm + part * part
        tload[g * 16 : (g + 1) * 16, :] = t.astype(BF16)
    half_norm = 0.5 * jnp.sum(norm, axis=1, keepdims=True)
    rowid = lax.broadcasted_iota(jnp.int32, (16, 128), 0)
    load_prior.wait()
    pri = jnp.ones((16, 128), F32)
    for k in range(12):
        pri = jnp.where(rowid == k, prior[k], pri)
    slot = x * 2 + yl
    offs[slot] = jnp.log(pri) - half_norm

    sub8 = lax.broadcasted_iota(jnp.int32, (8, 128), 0)

    def arrange(v, c):
        o = dot(tload[...], perm[:, pl.ds(pl.multiple_of(v * 128, 128), 128)])
        halves = [turn32([o[(2 * zz + h) * 16 : (2 * zz + h) * 16 + 16] for zz in range(4)]) for h in range(2)]
        rows = []
        for i in range(4):
            a, b = halves[0][i], halves[1][i]
            rows += [a[:8], b[:8], jnp.where(sub8 < 4, a[8:], pltpu.roll(b[8:], 4, 0))]
        tbuf[slot, pl.ds(pl.multiple_of(96 * v, 32), 96), :] = jnp.concatenate(rows, axis=0).astype(BF16)
        return c

    lax.fori_loop(0, 9, arrange, 0, unroll=9)

    pl.semaphore_wait(barrier, len(partners))

    PIECES = ((0, 224), (224, 208), (432, 224), (656, 208))

    def piece(s, p):
        return tbuf.at[s, pl.ds(*PIECES[p])]

    started = []

    def send(s, p, target, n):
        c = pltpu.make_async_remote_copy(
            piece(s, p), piece(s, p), send_sem.at[n], recv_sem.at[n], device_id=target, device_id_type=MESH
        )
        c.start()
        started.append(c)

    def arrived(s, p, n):
        pltpu.make_async_copy(piece(s, p), piece(s, p), recv_sem.at[n]).wait()

    for k in range(2):
        send(slot, k, to_xp, k)
        send(slot, 2 + k, to_xm, 6 + k)
        send(slot, k, to_yp, 12 + k)
        send(slot, 2 + k, to_ym, 14 + k)
    for k in range(2):
        send(slot, 2 + k, to_xp, 2 + k)
        send(slot, k, to_xm, 4 + k)
    off_copies = []
    for d in range(1, 8):
        c = pltpu.make_async_remote_copy(
            offs.at[slot], offs.at[slot], off_send.at[d], off_recv.at[d], device_id=away(d), device_id_type=MESH
        )
        c.start()
        off_copies.append(c)
    s_m, s_p, s_2 = xm * 2 + yl, xp * 2 + yl, x2 * 2 + yl
    o_0, o_m, o_p, o_2 = x * 2 + 1 - yl, xm * 2 + 1 - yl, xp * 2 + 1 - yl, x2 * 2 + 1 - yl

    load_images.wait()
    for g in range(3):
        cols = slice(g * 384, g * 384 + 384)
        stacked = jnp.concatenate([images[:, q * BAND : (q + 1) * BAND] for q in range(8)], axis=0)
        o = dot(stacked, perm[:, cols])
        parts = [o[q * 64 : q * 64 + 64] for q in range(8)]
        for vv in range(3):
            v = 3 * g + vv
            for h in range(2):
                t = turn32([parts[2 * zz + h][:, vv * 128 : vv * 128 + 128] for zz in range(4)])
                for i in range(4):
                    x5[core, 4 * v + i, :, h * 128 : h * 128 + 128] = t[i].astype(BF16)
    swap = pltpu.make_async_remote_copy(
        x5.at[core], x5.at[core], pair_send.at[0], pair_recv.at[0], device_id=sibling, device_id_type=MESH
    )
    swap.start()

    for k in range(2):
        arrived(s_m, k, k)
        send(s_m, k, to_xp, 8 + k)
        send(s_m, k, to_yp, 16 + k)
        arrived(s_p, 2 + k, 6 + k)
        send(s_p, 2 + k, to_xm, 10 + k)
        send(s_p, 2 + k, to_ym, 22 + k)

    def image_spectra(c):
        def step(n, carry):
            t, h = n // 2, n % 2
            r0 = pl.multiple_of(t * 16, 16)
            lanes = pl.ds(pl.multiple_of(h * 128, 128), 128)
            p = forward36([x5[c, b, pl.ds(r0, 16), lanes].astype(F32) for b in range(36)])
            for f in range(HALF):
                for ri in range(2):
                    a, b = split(p[f][ri])
                    at = pl.ds(pl.multiple_of(ri * 128 + c * 64 + r0, 16), 16)
                    xh[f, 0, at, lanes] = a
                    xh[f, 1, at, lanes] = b
            return carry

        lax.fori_loop(0, 8, step, 0)

    image_spectra(core)
    for k in range(2):
        arrived(s_p, k, 4 + k)
        send(s_p, k, to_yp, 20 + k)
        arrived(s_m, 2 + k, 2 + k)
        send(s_m, 2 + k, to_ym, 18 + k)
    swap.wait()
    image_spectra(1 - core)
    for k in range(2):
        arrived(s_2, k, 8 + k)
        send(s_2, k, to_yp, 24 + k)
        arrived(s_2, 2 + k, 10 + k)
        send(s_2, 2 + k, to_ym, 26 + k)

    def distance(i):
        return jnp.where(i == 3, 2, jnp.where(i == 2, 3, i))

    def row(i, part):
        return jnp.where(i == 3, 72 + 8 * part, 24 * part + 8 * i)

    def template_spectra(i, ll):
        s = (x + distance(i)) % 4 * 2 + ll
        raw = []
        for b in range(HALF):
            two = tbuf[s, 48 * b : 48 * b + 48, :].astype(F32)
            raw += [two[:24], two[24:]]
        p = forward36(raw)
        at = pl.ds(pl.multiple_of(row(i, ll), 8), 8)
        for f in range(HALF):
            for ri in range(2):
                v = p[f][ri]
                tf[f, ri, at, 0:128] = v[0:8]
                tf[f, ri, at, 128:256] = v[8:16]
                tmix[i, ll, f, ri] = v[16:24]

    def score_part(members, lo, hi):
        count = hi - lo

        def score(f, c):
            for ri in range(2):
                for i in members:
                    a, b = tmix[i, 0, f, ri], tmix[i, 1, f, ri]
                    at = 88 if i == 3 else 48 + 8 * i
                    tf[f, ri, at : at + 8, 0:128] = jnp.where(sub8 < 4, a, pltpu.roll(b, 4, 0))
                    tf[f, ri, at : at + 8, 128:256] = jnp.where(sub8 < 4, pltpu.roll(a, 4, 0), b)
            high, low = split(jnp.concatenate([tf[f, 0, lo:hi, :], tf[f, 1, lo:hi, :]], axis=0))
            m = dot(high, xh[f, 0], NT) + (dot(low, xh[f, 0], NT) + dot(high, xh[f, 1], NT))
            rr, ri_, ir, ii = m[:count, :128], m[:count, 128:], m[count:, :128], m[count:, 128:]
            first = f == 0
            sh[2 * f, lo:hi, :] = jnp.where(first, rr, rr + ii)
            sh[2 * f + 1, lo:hi, :] = jnp.where(first, ii, ri_ - ir)
            return c

        lax.fori_loop(0, HALF, score, 0, unroll=6)

    def own_row(i, c):
        template_spectra(i, yl)
        return c

    def other_row(i, c):
        template_spectra(i, 1 - yl)
        return c

    lax.fori_loop(0, 4, own_row, 0)
    for p in range(4):
        arrived(o_0, p, 12 + p)
    for p in range(4):
        arrived(o_m, p, 16 + p)
        arrived(o_p, p, 20 + p)
    lax.fori_loop(0, 3, other_row, 0)
    for p in range(4):
        arrived(o_2, p, 24 + p)
    lax.fori_loop(3, 4, other_row, 0)
    score_part((0, 1, 2, 3), 0, 96)
    for c in off_copies:
        c.wait()

    def to_turns(off, rows, top):
        p = [(sh[2 * f, rows, :], sh[2 * f + 1, rows, :]) for f in range(HALF)]
        s = inverse36(p)
        for r in range(36):
            v = s[r] * (1.0 / 36.0) + off
            sh[r, rows, :] = v
            top = jnp.maximum(top, v)
        return top

    def rows_of(n, c):
        i = jnp.where(n < 9, n % 3, 3)
        part = jnp.where(n < 9, n // 3, n - 9)
        at = (x + distance(i)) % 4 * 2
        a, b = offs[at], offs[at + 1]
        last = jnp.where(sub8 < 4, a[8:], pltpu.roll(b[8:], 4, 0))
        off = jnp.where(part == 0, a[:8], jnp.where(part == 1, b[:8], last))
        return to_turns(off, pl.ds(pl.multiple_of(n * 8, 8), 8), c)

    top8 = lax.fori_loop(0, 12, rows_of, jnp.full((8, 128), -jnp.inf, F32))
    top = jnp.max(top8, axis=0, keepdims=True)

    def raise_(n, c):
        rows = pl.ds(pl.multiple_of(n * 8, 8), 8)
        for r in range(36):
            e = jnp.exp(sh[r, rows, :] - top)
            sh[r, rows, :] = e
            c = c + e
        return c

    total = jnp.sum(lax.fori_loop(0, 12, raise_, jnp.zeros((8, 128), F32)), axis=0, keepdims=True)
    stat[0, 0] = jnp.broadcast_to(top, (8, 128))
    stat[0, 1] = jnp.broadcast_to(total, (8, 128))
    share = pltpu.make_async_remote_copy(
        stat.at[0], stat.at[1], pair_send.at[1], pair_recv.at[1], device_id=sibling, device_id_type=MESH
    )
    share.start()
    share.wait()
    top_o, total_o = stat[1, 0][:1], stat[1, 1][:1]
    peak = jnp.maximum(top, top_o)
    mine = jnp.exp(top - peak)
    scale = mine / (total * mine + total_o * jnp.exp(top_o - peak))

    def weigh(n, c):
        rows = pl.ds(pl.multiple_of(n * 16, 16), 16)
        upper = pl.ds(pl.multiple_of(n * 16 + 96, 16), 16)
        w = [(sh[r, rows, :] * scale).astype(BF16).astype(F32) for r in range(36)]
        p = forward36(w)
        mass[rows, :] = jnp.broadcast_to(jnp.sum(p[0][0], axis=1, keepdims=True), (16, 128))
        none = jnp.zeros((16, 128), BF16)
        for f in range(HALF):
            for part, (r, i) in enumerate(zip(split(p[f][0]), split(p[f][1]))):
                lh[f, part, rows, 0:128] = r
                lh[f, part, rows, 128:256] = none if f == 0 else i
                lh[f, part, upper, 0:128] = none if f == 0 else -i
                lh[f, part, upper, 128:256] = i if f == 0 else r
        return c

    lax.fori_loop(0, 6, weigh, 0)

    def sums(u, c):
        comps = []
        for ff in range(2):
            f = 2 * u + ff
            a, b = lh[f, 0], lh[f, 1]
            m = dot(a, xh[f, 0]) + (dot(b, xh[f, 0]) + dot(a, xh[f, 1]))
            comps += [m[:96], m[96:]]
        at = pl.ds(pl.multiple_of(8 * u, 8), 8)
        for h in range(2):
            t = turn32([v[:, h * 128 : h * 128 + 128] for v in comps])
            for zz in range(4):
                for i in range(4):
                    xx = (x + (0, 1, 3, 2)[i]) % 4
                    r = [72 + 8 * p if i == 3 else 24 * p + 8 * i for p in range(3)]
                    cf[zz, h, xx, 0, at, :] = t[zz][r[0] : r[0] + 8]
                    cf[zz, h, xx, 1, at, :] = t[zz][r[1] : r[1] + 8]
                    cmix[zz, h, xx, u] = t[zz][r[2] : r[2] + 8]
        return c

    place = (x, y, z)
    copies = []

    ORDER = (2, 1, 3, 0)

    def go(n, axis, r, src, dst):
        c = pltpu.make_async_remote_copy(
            src, dst, rs_send.at[n], rs_recv.at[n], device_id=along(axis, r), device_id_type=MESH
        )
        c.start()
        copies.append(c)
        return c

    def first_stage(share, axis, second, src, dst):
        groups = {}
        for k in ORDER:
            to = (place[second] + k) % 4
            groups[k] = [
                go(12 * share + 3 * k + r - 1, axis, r, src.at[(place[axis] + r) % 4, to], dst.at[r, to])
                for r in range(1, 4)
            ]
        return groups

    def landed(group):
        for c in group:
            c.wait_recv()

    def rows_a(zz, hh, xx, ll):
        return cf[zz, hh, xx, ll, 0:48, :]

    def pack_a(n, c):
        zz, hh, xx = n // 8, (n // 4) % 2, n % 4
        for ll in range(2):
            s1a[xx, 2 * hh + ll, zz] = rows_a(zz, hh, xx, ll).astype(BF16)
        return c

    l8 = lane((8, 128)) // 16

    def rows_bc(zz, hh, xx):
        mixes = [cmix[zz, hh, xx, u] for u in range(9)]
        tails = ([], [])
        for u in range(0, 8, 2):
            a, b = mixes[u], mixes[u + 1]
            tails[0].append(jnp.where(sub8 < 4, a, pltpu.roll(b, 4, 0)))
            tails[1].append(jnp.where(sub8 < 4, pltpu.roll(a, 4, 0), b))
        d = (xx - x + 4) % 4
        i = distance(d)
        m0, m1, mm = (mass[pl.ds(pl.multiple_of(row(i, p), 8), 8), :] for p in range(3))
        for ll, (m8, m4, last) in enumerate(
            ((m0, pltpu.roll(mm, 4, 0), mixes[8]), (m1, mm, pltpu.roll(mixes[8], 4, 0)))
        ):
            v = jnp.where(l8 < 2, pltpu.roll(m8, 4, 0), jnp.where(l8 < 4, m8, m4))
            vh = v.astype(BF16).astype(F32)
            v = jnp.where(l8 % 2 == 0, vh, v - vh)
            tails[ll].append(jnp.where(sub8 < 4, last, v))
        return [
            (
                jnp.concatenate([cf[zz, hh, xx, ll, 48:72, :], tails[ll][0]], axis=0),
                jnp.concatenate(tails[ll][1:], axis=0),
            )
            for ll in range(2)
        ]

    def pack_bc(n, c):
        zz, hh, xx = n // 8, (n // 4) % 2, n % 4
        for ll, (b, c_) in enumerate(rows_bc(zz, hh, xx)):
            s1b[2 * hh + ll, zz, xx] = b.astype(BF16)
            s1c[zz, xx, 2 * hh + ll] = c_.astype(BF16)
        return c

    lax.fori_loop(0, 6, sums, 0, unroll=3)
    lax.fori_loop(0, 32, pack_a, 0)
    g1a = first_stage(0, 0, 1, s1a, r1a)
    lax.fori_loop(6, 9, sums, 0, unroll=3)
    lax.fori_loop(0, 32, pack_bc, 0)
    g1b = first_stage(1, 1, 2, s1b, r1b)
    g1c = first_stage(2, 2, 0, s1c, r1c)

    def keep_a(n, c):
        for ll in range(2):
            own_a[2 * (n % 2) + ll, n // 2] = rows_a(n // 2, n % 2, x, ll)
        return c

    def keep_b(n, c):
        both = rows_bc(n // 4, yh, n % 4)
        own_b[n // 4, n % 4] = jnp.where(yl == 0, both[0][0], both[1][0])
        return c

    def keep_c(n, c):
        for ll, (_, v) in enumerate(rows_bc(z, n // 4, n % 4)):
            own_c[n % 4, 2 * (n // 4) + ll] = v
        return c

    lax.fori_loop(0, 8, keep_a, 0)
    lax.fori_loop(0, 16, keep_b, 0)
    lax.fori_loop(0, 8, keep_c, 0)

    shares = (
        (g1a, own_a, r1a, s2a, r2a, s3a, r3a, 1, 2),
        (g1b, own_b, r1b, s2b, r2b, s3b, r3b, 2, 0),
        (g1c, own_c, r1c, s2c, r2c, s3c, r3c, 0, 1),
    )
    g2 = ([], [], [])
    for k in ORDER:
        for share, (g1, own, r1, s2, r2, s3, r3, second, third) in enumerate(shares):
            landed(g1[k])
            to = (place[second] + k) % 4
            for j in range(4):
                total = own[to, j] + (r1[1, to, j].astype(F32) + r1[2, to, j].astype(F32)) + r1[3, to, j].astype(F32)
                if k:
                    s2[to, j] = total.astype(BF16)
                else:
                    own[to, j] = total
            if k:
                g2[share].append(go(36 + 3 * share + k - 1, second, k, s2.at[to], r2.at[k]))
    g3 = []
    for share, (g1, own, r1, s2, r2, s3, r3, second, third) in enumerate(shares):
        landed(g2[share])
        for j in range(4):
            s3[j] = own[place[second], j] + (r2[1, j].astype(F32) + r2[2, j].astype(F32)) + r2[3, j].astype(F32)
        g3.append(
            [
                go(45 + 3 * share + k - 1, third, k, s3.at[(place[third] + k) % 4], r3.at[k])
                for k in range(1, 4)
            ]
        )

    def add_third(held, got, axis):
        return held[place[axis]] + (got[1] + got[2]) + got[3]

    g3a, g3b, g3c = g3
    landed(g3a)
    part_a = add_third(s3a, r3a, 2)
    landed(g3b)
    part_b = add_third(s3b, r3b, 0)
    landed(g3c)
    part_c = add_third(s3c, r3c, 1)

    v = jnp.concatenate([part_a, part_b, part_c], axis=0)
    pairs = []
    for u in range(9):
        tail = v[72 + 8 * (u // 2) : 80 + 8 * (u // 2)]
        if u % 2:
            tail = pltpu.roll(tail, 4, 0)
        both = jnp.concatenate([v[8 * u : 8 * u + 8], tail], axis=0)
        comps = [both] + [pltpu.roll(both, 128 - 32 * i, 1) for i in range(1, 4)]
        pairs += [(comps[0], comps[1]), (comps[2], comps[3])]
    s = [w * (1.0 / 36.0) for w in inverse36(pairs)]
    block = lane((16, 128)) // 32
    cols = []
    for b in range(0, 36, 4):
        w = s[b]
        for i in range(1, 4):
            w = jnp.where(block == i, pltpu.roll(s[b + i], 32 * i, 1), w)
        cols.append(w)
    high, low = split(jnp.concatenate(cols, axis=1))
    o = dot(jnp.concatenate([high, low], axis=0), perm[...], NT)
    out[...] = (o[:16] + o[16:])[:12]
    m = v[104:112]
    m = m + pltpu.roll(m, 112, 1)
    l128 = lane((8, 128))
    for k in range(12):
        out_mass[k] = jnp.sum(jnp.where((sub8 == 4 + k % 4) & (l128 == 32 * (k // 4)), m, 0.0))
    for c in copies:
        c.wait_send()
    for c in started:
        c.wait_send()


def per_device(images, references, class_prior):
    hbm = pl.BlockSpec(memory_space=pl.ANY)
    smem = pl.BlockSpec(memory_space=pltpu.SMEM)
    rows = (48, 32, 32)
    return pl.pallas_call(
        kernel,
        out_shape=(jax.ShapeDtypeStruct((12, BAND), F32), jax.ShapeDtypeStruct((12,), F32)),
        in_specs=[hbm, hbm, hbm],
        out_specs=(pl.BlockSpec(memory_space=pltpu.VMEM), smem),
        scratch_shapes=[
            pltpu.SMEM((12,), F32),
            pltpu.VMEM((64, 9216), BF16),
            pltpu.VMEM((BAND, BAND), BF16),
            pltpu.VMEM((12, 16, 9216), BF16),
            pltpu.VMEM((128, BAND), BF16),
            pltpu.VMEM((2, 36, 64, 256), BF16),
            pltpu.VMEM((HALF, 2, 256, 256), BF16),
            pltpu.VMEM((8, 864, 128), BF16),
            pltpu.VMEM((HALF, 2, 96, 256), F32),
            pltpu.VMEM((4, 2, HALF, 2, 8, 128), F32),
            pltpu.VMEM((8, 16, 128), F32),
            pltpu.VMEM((36, 96, 128), F32),
            pltpu.VMEM((2, 2, 8, 128), F32),
            pltpu.VMEM((HALF, 2, 192, 256), BF16),
            pltpu.VMEM((96, 128), F32),
            pltpu.VMEM((4, 2, 4, 2, 72, 128), F32),
            pltpu.VMEM((4, 2, 4, 9, 8, 128), F32),
            *[pltpu.VMEM((4, 4, r, 128), F32) for r in rows],
            *[pltpu.VMEM((4, 4, 4, r, 128), BF16) for r in rows],
            *[pltpu.VMEM((4, 4, 4, r, 128), BF16) for r in rows],
            *[pltpu.VMEM((4, 4, r, 128), BF16) for r in rows],
            *[pltpu.VMEM((4, 4, r, 128), BF16) for r in rows],
            *[pltpu.VMEM((4, r, 128), F32) for r in rows],
            *[pltpu.VMEM((4, r, 128), F32) for r in rows],
            pltpu.SemaphoreType.DMA((14,)),
            pltpu.SemaphoreType.DMA((28,)),
            pltpu.SemaphoreType.DMA((28,)),
            pltpu.SemaphoreType.DMA((8,)),
            pltpu.SemaphoreType.DMA((8,)),
            pltpu.SemaphoreType.DMA((2,)),
            pltpu.SemaphoreType.DMA((2,)),
            pltpu.SemaphoreType.DMA((54,)),
            pltpu.SemaphoreType.DMA((54,)),
        ],
        compiler_params=pltpu.CompilerParams(
            collective_id=0, has_side_effects=True, vmem_limit_bytes=56 * 1024 * 1024
        ),
        name="em_pass",
    )(class_prior, images, references)


def solution(mesh):
    placed = (P(("img", "ref"), None), P("ref", None), P("ref"))
    return jax.shard_map(
        per_device,
        mesh=mesh,
        in_specs=placed,
        out_specs=(P("ref", "img"), P("ref")),
        check_vma=False,
    )
```

```python
import math
import jax
import jax.numpy as jnp
from jax import lax
from jax.experimental import pallas as pl
from jax.experimental.pallas import tpu as pltpu
from jax.sharding import PartitionSpec as P

ANG = 144
ROT = 36
TURN = 4
BAND = 1152
HALF = ROT // 2
F32 = jnp.float32
BF16 = jnp.bfloat16
MESH = pl.DeviceIdType.MESH

COS9 = [math.cos(2 * math.pi * m / 9) for m in range(9)]
SIN9 = [math.sin(2 * math.pi * m / 9) for m in range(9)]
ROOT3H = math.sqrt(3.0) / 2


def cos_sums(y0, e):
    t = e[0] + e[1] + e[3]
    top = y0 + e[2]
    base = y0 - 0.5 * e[2]
    out = [top + t]
    for f in (1, 2, 4):
        out.append(base + COS9[f % 9] * e[0] + COS9[2 * f % 9] * e[1] + COS9[4 * f % 9] * e[3])
    out.insert(3, top - 0.5 * t)
    return out


def sin_sums(o):
    h = ROOT3H * o[2]
    one = SIN9[1] * o[0] + SIN9[2] * o[1] + h + SIN9[4] * o[3]
    two = SIN9[2] * o[0] + SIN9[4] * o[1] - h - SIN9[1] * o[3]
    three = ROOT3H * (o[0] - o[1] + o[3])
    four = SIN9[4] * o[0] - SIN9[1] * o[1] + h - SIN9[2] * o[3]
    return [one, two, three, four]


def real9(y):
    e = [y[m] + y[9 - m] for m in range(1, 5)]
    o = [y[m] - y[9 - m] for m in range(1, 5)]
    s = sin_sums(o)
    return cos_sums(y[0], e), [None] + [-v for v in s]


def forward36(x):
    y0, y2, y1r, y1i = [], [], [], []
    for b2 in range(9):
        x0, x1, x2, x3 = (x[(9 * b1 + 4 * b2) % 36] for b1 in range(4))
        u0, u1, v0, v1 = x0 + x2, x0 - x2, x1 + x3, x3 - x1
        y0.append(u0 + v0)
        y2.append(u0 - v0)
        y1r.append(u1)
        y1i.append(v1)
    z0r, z0i = real9(y0)
    z2r, z2i = real9(y2)
    ur, ui = real9(y1r)
    vr, vi = real9(y1i)
    z1r, z1i = [None] * 9, [None] * 9
    z1r[0], z1i[0] = ur[0], vr[0]
    for f in range(1, 5):
        z1r[f], z1i[f] = ur[f] - vi[f], ui[f] + vr[f]
        z1r[9 - f], z1i[9 - f] = ur[f] + vi[f], vr[f] - ui[f]

    def at(f):
        f1, f2 = f % 4, f % 9
        if f1 in (0, 2):
            r, i = (z0r, z0i) if f1 == 0 else (z2r, z2i)
            if f2 == 0:
                return r[0], None
            return (r[f2], i[f2]) if f2 <= 4 else (r[9 - f2], -i[9 - f2])
        if f1 == 1:
            return z1r[f2], z1i[f2]
        g = (9 - f2) % 9
        return z1r[g], -z1i[g]

    return [(at(0)[0], at(18)[0])] + [at(f) for f in range(1, HALF)]


def inverse36(pairs):
    def spec(f):
        f %= 36
        if f == 0:
            return pairs[0][0], None
        if f == 18:
            return pairs[0][1], None
        if f < 18:
            return pairs[f]
        r, i = pairs[36 - f]
        return r, -i

    def find(f1, f2):
        return spec(next(f for f in range(36) if f % 4 == f1 and f % 9 == f2))

    def hermitian(f1):
        r0 = find(f1, 0)[0]
        z = [find(f1, f) for f in range(1, 5)]
        c = cos_sums(r0, [2.0 * r for r, _ in z])
        s = sin_sums([2.0 * i for _, i in z])
        y = [None] * 9
        y[0] = c[0]
        for m in range(1, 5):
            y[m], y[9 - m] = c[m] - s[m - 1], c[m] + s[m - 1]
        return y

    y0, y2 = hermitian(0), hermitian(2)
    z = [find(1, f) for f in range(9)]
    er = [z[f][0] + z[9 - f][0] for f in range(1, 5)]
    ei = [z[f][1] + z[9 - f][1] for f in range(1, 5)]
    dr = [z[f][0] - z[9 - f][0] for f in range(1, 5)]
    di = [z[f][1] - z[9 - f][1] for f in range(1, 5)]
    cr, ci = cos_sums(z[0][0], er), cos_sums(z[0][1], ei)
    sr, si = sin_sums(dr), sin_sums(di)
    y1r, y1i = [cr[0]] + [None] * 8, [ci[0]] + [None] * 8
    for m in range(1, 5):
        y1r[m], y1r[9 - m] = cr[m] - si[m - 1], cr[m] + si[m - 1]
        y1i[m], y1i[9 - m] = ci[m] + sr[m - 1], ci[m] - sr[m - 1]
    x = [None] * 36
    for b2 in range(9):
        p, q = y0[b2] + y2[b2], y0[b2] - y2[b2]
        a, b = 2.0 * y1r[b2], 2.0 * y1i[b2]
        for b1, v in enumerate((p + a, q - b, p - a, q + b)):
            x[(9 * b1 + 4 * b2) % 36] = v
    return x


def lane(shape):
    return lax.broadcasted_iota(jnp.int32, shape, len(shape) - 1)


def turn32(a):
    l = lane(a[0].shape)
    low = l < 64
    even = (l // 32) % 2 == 0
    b0 = jnp.where(low, a[0], pltpu.roll(a[2], 64, 1))
    b2 = jnp.where(low, pltpu.roll(a[0], 64, 1), a[2])
    b1 = jnp.where(low, a[1], pltpu.roll(a[3], 64, 1))
    b3 = jnp.where(low, pltpu.roll(a[1], 64, 1), a[3])
    out = []
    for p, q in ((b0, b1), (b2, b3)):
        out.append(jnp.where(even, p, pltpu.roll(q, 32, 1)))
        out.append(jnp.where(even, pltpu.roll(p, 96, 1), q))
    return out


def split(v):
    h = v.astype(BF16)
    return h, (v - h.astype(F32)).astype(BF16)


NT = (((1,), (1,)), ((), ()))
NN = (((1,), (0,)), ((), ()))


def dot(a, b, dims=NN):
    return lax.dot_general(a, b, dims, preferred_element_type=F32)


def kernel(
    prior_hbm, images_hbm, refs, out, out_mass,
    prior, images, perm, rows16, tload, x5, xh, tbuf, tf, tmix, offs, sh, stat, lh, mass, cf, cmix,
    own_a, own_b, own_c, s1a, s1b, s1c, r1a, r1b, r1c, s2a, s2b, s2c, r2a, r2b, r2c, s3a, s3b, s3c, r3a, r3b, r3c,
    load_sem, send_sem, recv_sem, off_send, off_recv, pair_send, pair_recv, rs_send, rs_recv,
):
    img, ref = lax.axis_index("img"), lax.axis_index("ref")
    z, yh = img // 2, img % 2
    x, yl, core = ref // 4, (ref // 2) % 2, ref % 2

    def dev(x_, y_, z_, c_):
        return {"img": z_ * 2 + y_ // 2, "ref": x_ * 4 + (y_ % 2) * 2 + c_}

    y = yh * 2 + yl
    xp, xm = (x + 1) % 4, (x + 3) % 4
    x2 = (x + 2) % 4
    to_xp, to_xm = dev(xp, y, z, core), dev(xm, y, z, core)
    to_yp, to_ym = dev(x, (y + 1) % 4, z, core), dev(x, (y + 3) % 4, z, core)
    sibling = dev(x, y, z, 1 - core)

    loads = []
    for k in range(12):
        c = pltpu.make_async_copy(refs.at[pl.ds(36 * k // 16 * 16, 16)], rows16.at[k], load_sem.at[k])
        c.start()
        loads.append(c)
    load_prior = pltpu.make_async_copy(prior_hbm, prior, load_sem.at[12])
    load_prior.start()
    load_images = pltpu.make_async_copy(images_hbm, images, load_sem.at[13])
    load_images.start()

    def along(axis, r):
        x_, y_, z_ = ((v + r * (a == axis)) % 4 for a, v in enumerate((x, y, z)))
        return dev(x_, y_, z_, core)

    def away(d):
        return dev((x + d // 2) % 4, yh * 2 + (yl + d) % 2, z, core)

    barrier = pltpu.get_barrier_semaphore()
    partners = [along(a, r) for a in range(3) for r in range(1, 4)] + [away(d) for d in (3, 5, 7)] + [sibling]
    for p in partners:
        pl.semaphore_signal(barrier, inc=1, device_id=p, device_id_type=MESH)
    def permutation(n, c):
        i = n * 128 + lax.broadcasted_iota(jnp.int32, (128, 128), 0)
        cycle = jnp.zeros_like(i)
        for q in range(1, 8):
            cycle = cycle + jnp.where(i >= ANG * q, 1, 0)
        i = i - ANG * cycle
        to = (i >> 2) * 32 + cycle * 4 + (i & 3) - lane((128, 128))
        for v in range(9):
            perm[pl.ds(pl.multiple_of(n * 128, 128), 128), v * 128 : v * 128 + 128] = jnp.where(
                to == 128 * v, 1.0, 0.0
            ).astype(BF16)
        return c

    lax.fori_loop(0, 9, permutation, 0)

    for c in loads:
        c.wait()
    norm = jnp.zeros((16, 128), F32)
    for g in range(8):
        tiles = []
        for k in range(12):
            at = 36 * k % 16
            tiles.append(rows16[k, :, g * BAND : (g + 1) * BAND].astype(F32)[at : at + 1])
        tiles.append(jnp.zeros((4, BAND), F32))
        t = jnp.concatenate(tiles, axis=0)
        for v in range(9):
            part = t[:, v * 128 : (v + 1) * 128]
            norm = norm + part * part
        tload[g * 16 : (g + 1) * 16, :] = t.astype(BF16)
    half_norm = 0.5 * jnp.sum(norm, axis=1, keepdims=True)
    rowid = lax.broadcasted_iota(jnp.int32, (16, 128), 0)
    load_prior.wait()
    pri = jnp.ones((16, 128), F32)
    for k in range(12):
        pri = jnp.where(rowid == k, prior[k], pri)
    slot = x * 2 + yl
    offs[slot] = jnp.log(pri) - half_norm

    sub8 = lax.broadcasted_iota(jnp.int32, (8, 128), 0)

    def arrange(v, c):
        o = dot(tload[...], perm[:, pl.ds(pl.multiple_of(v * 128, 128), 128)])
        halves = [turn32([o[(2 * zz + h) * 16 : (2 * zz + h) * 16 + 16] for zz in range(4)]) for h in range(2)]
        rows = []
        for i in range(4):
            a, b = halves[0][i], halves[1][i]
            rows += [a[:8], b[:8], jnp.where(sub8 < 4, a[8:], pltpu.roll(b[8:], 4, 0))]
        tbuf[slot, pl.ds(pl.multiple_of(96 * v, 32), 96), :] = jnp.concatenate(rows, axis=0).astype(BF16)
        return c

    lax.fori_loop(0, 9, arrange, 0, unroll=9)

    pl.semaphore_wait(barrier, len(partners))

    PIECES = ((0, 224), (224, 208), (432, 224), (656, 208))

    def piece(s, p):
        return tbuf.at[s, pl.ds(*PIECES[p])]

    started = []

    def send(s, p, target, n):
        c = pltpu.make_async_remote_copy(
            piece(s, p), piece(s, p), send_sem.at[n], recv_sem.at[n], device_id=target, device_id_type=MESH
        )
        c.start()
        started.append(c)

    def arrived(s, p, n):
        pltpu.make_async_copy(piece(s, p), piece(s, p), recv_sem.at[n]).wait()

    for k in range(2):
        send(slot, k, to_xp, k)
        send(slot, 2 + k, to_xm, 6 + k)
        send(slot, k, to_yp, 12 + k)
        send(slot, 2 + k, to_ym, 14 + k)
    for k in range(2):
        send(slot, 2 + k, to_xp, 2 + k)
        send(slot, k, to_xm, 4 + k)
    off_copies = []
    for d in range(1, 8):
        c = pltpu.make_async_remote_copy(
            offs.at[slot], offs.at[slot], off_send.at[d], off_recv.at[d], device_id=away(d), device_id_type=MESH
        )
        c.start()
        off_copies.append(c)
    s_m, s_p, s_2 = xm * 2 + yl, xp * 2 + yl, x2 * 2 + yl
    o_0, o_m, o_p, o_2 = x * 2 + 1 - yl, xm * 2 + 1 - yl, xp * 2 + 1 - yl, x2 * 2 + 1 - yl

    load_images.wait()
    for g in range(3):
        cols = slice(g * 384, g * 384 + 384)
        stacked = jnp.concatenate([images[:, q * BAND : (q + 1) * BAND] for q in range(8)], axis=0)
        o = dot(stacked, perm[:, cols])
        parts = [o[q * 64 : q * 64 + 64] for q in range(8)]
        for vv in range(3):
            v = 3 * g + vv
            for h in range(2):
                t = turn32([parts[2 * zz + h][:, vv * 128 : vv * 128 + 128] for zz in range(4)])
                for i in range(4):
                    x5[core, 4 * v + i, :, h * 128 : h * 128 + 128] = t[i].astype(BF16)
    swap = pltpu.make_async_remote_copy(
        x5.at[core], x5.at[core], pair_send.at[0], pair_recv.at[0], device_id=sibling, device_id_type=MESH
    )
    swap.start()

    for k in range(2):
        arrived(s_m, k, k)
        send(s_m, k, to_xp, 8 + k)
        send(s_m, k, to_yp, 16 + k)
        arrived(s_p, 2 + k, 6 + k)
        send(s_p, 2 + k, to_xm, 10 + k)
        send(s_p, 2 + k, to_ym, 22 + k)

    def image_spectra(c):
        def step(n, carry):
            t, h = n // 2, n % 2
            r0 = pl.multiple_of(t * 16, 16)
            lanes = pl.ds(pl.multiple_of(h * 128, 128), 128)
            p = forward36([x5[c, b, pl.ds(r0, 16), lanes].astype(F32) for b in range(36)])
            for f in range(HALF):
                for ri in range(2):
                    a, b = split(p[f][ri])
                    at = pl.ds(pl.multiple_of(ri * 128 + c * 64 + r0, 16), 16)
                    xh[f, 0, at, lanes] = a
                    xh[f, 1, at, lanes] = b
            return carry

        lax.fori_loop(0, 8, step, 0)

    image_spectra(core)
    for k in range(2):
        arrived(s_p, k, 4 + k)
        send(s_p, k, to_yp, 20 + k)
        arrived(s_m, 2 + k, 2 + k)
        send(s_m, 2 + k, to_ym, 18 + k)
    swap.wait()
    image_spectra(1 - core)
    for k in range(2):
        arrived(s_2, k, 8 + k)
        send(s_2, k, to_yp, 24 + k)
        arrived(s_2, 2 + k, 10 + k)
        send(s_2, 2 + k, to_ym, 26 + k)

    def distance(i):
        return jnp.where(i == 3, 2, jnp.where(i == 2, 3, i))

    def row(i, part):
        return jnp.where(i == 3, 72 + 8 * part, 24 * part + 8 * i)

    def template_spectra(i, ll):
        s = (x + distance(i)) % 4 * 2 + ll
        raw = []
        for b in range(HALF):
            two = tbuf[s, 48 * b : 48 * b + 48, :].astype(F32)
            raw += [two[:24], two[24:]]
        p = forward36(raw)
        at = pl.ds(pl.multiple_of(row(i, ll), 8), 8)
        for f in range(HALF):
            for ri in range(2):
                v = p[f][ri]
                tf[f, ri, at, 0:128] = v[0:8]
                tf[f, ri, at, 128:256] = v[8:16]
                tmix[i, ll, f, ri] = v[16:24]

    def score_part(members, lo, hi):
        count = hi - lo

        def score(f, c):
            for ri in range(2):
                for i in members:
                    a, b = tmix[i, 0, f, ri], tmix[i, 1, f, ri]
                    at = 88 if i == 3 else 48 + 8 * i
                    tf[f, ri, at : at + 8, 0:128] = jnp.where(sub8 < 4, a, pltpu.roll(b, 4, 0))
                    tf[f, ri, at : at + 8, 128:256] = jnp.where(sub8 < 4, pltpu.roll(a, 4, 0), b)
            high, low = split(jnp.concatenate([tf[f, 0, lo:hi, :], tf[f, 1, lo:hi, :]], axis=0))
            m = dot(jnp.concatenate([high, low], axis=0), xh[f, 0], NT)
            m = m[: 2 * count] + (m[2 * count :] + dot(high, xh[f, 1], NT))
            rr, ri_, ir, ii = m[:count, :128], m[:count, 128:], m[count:, :128], m[count:, 128:]
            first = f == 0
            sh[2 * f, lo:hi, :] = jnp.where(first, rr, rr + ii)
            sh[2 * f + 1, lo:hi, :] = jnp.where(first, ii, ri_ - ir)
            return c

        lax.fori_loop(0, HALF, score, 0, unroll=6)

    def own_row(i, c):
        template_spectra(i, yl)
        return c

    def other_row(i, c):
        template_spectra(i, 1 - yl)
        return c

    lax.fori_loop(0, 4, own_row, 0)
    for p in range(4):
        arrived(o_0, p, 12 + p)
    for p in range(4):
        arrived(o_m, p, 16 + p)
        arrived(o_p, p, 20 + p)
    lax.fori_loop(0, 3, other_row, 0)
    for p in range(4):
        arrived(o_2, p, 24 + p)
    lax.fori_loop(3, 4, other_row, 0)
    score_part((0, 1, 2, 3), 0, 96)
    for c in off_copies:
        c.wait()

    def to_turns(off, rows, top):
        p = [(sh[2 * f, rows, :], sh[2 * f + 1, rows, :]) for f in range(HALF)]
        s = inverse36(p)
        for r in range(36):
            v = s[r] * (1.0 / 36.0) + off
            sh[r, rows, :] = v
            top = jnp.maximum(top, v)
        return top

    def rows_of(n, c):
        i = jnp.where(n < 9, n % 3, 3)
        part = jnp.where(n < 9, n // 3, n - 9)
        at = (x + distance(i)) % 4 * 2
        a, b = offs[at], offs[at + 1]
        last = jnp.where(sub8 < 4, a[8:], pltpu.roll(b[8:], 4, 0))
        off = jnp.where(part == 0, a[:8], jnp.where(part == 1, b[:8], last))
        return to_turns(off, pl.ds(pl.multiple_of(n * 8, 8), 8), c)

    top8 = lax.fori_loop(0, 12, rows_of, jnp.full((8, 128), -jnp.inf, F32))
    top = jnp.max(top8, axis=0, keepdims=True)

    def raise_(n, c):
        rows = pl.ds(pl.multiple_of(n * 8, 8), 8)
        for r in range(36):
            e = jnp.exp(sh[r, rows, :] - top)
            sh[r, rows, :] = e
            c = c + e
        return c

    total = jnp.sum(lax.fori_loop(0, 12, raise_, jnp.zeros((8, 128), F32)), axis=0, keepdims=True)
    stat[0, 0] = jnp.broadcast_to(top, (8, 128))
    stat[0, 1] = jnp.broadcast_to(total, (8, 128))
    share = pltpu.make_async_remote_copy(
        stat.at[0], stat.at[1], pair_send.at[1], pair_recv.at[1], device_id=sibling, device_id_type=MESH
    )
    share.start()
    share.wait()
    top_o, total_o = stat[1, 0][:1], stat[1, 1][:1]
    peak = jnp.maximum(top, top_o)
    mine = jnp.exp(top - peak)
    scale = mine / (total * mine + total_o * jnp.exp(top_o - peak))

    def weigh(n, c):
        rows = pl.ds(pl.multiple_of(n * 16, 16), 16)
        upper = pl.ds(pl.multiple_of(n * 16 + 96, 16), 16)
        w = [(sh[r, rows, :] * scale).astype(BF16).astype(F32) for r in range(36)]
        p = forward36(w)
        mass[rows, :] = jnp.broadcast_to(jnp.sum(p[0][0], axis=1, keepdims=True), (16, 128))
        none = jnp.zeros((16, 128), BF16)
        for f in range(HALF):
            for part, (r, i) in enumerate(zip(split(p[f][0]), split(p[f][1]))):
                lh[f, part, rows, 0:128] = r
                lh[f, part, rows, 128:256] = none if f == 0 else i
                lh[f, part, upper, 0:128] = none if f == 0 else -i
                lh[f, part, upper, 128:256] = i if f == 0 else r
        return c

    lax.fori_loop(0, 6, weigh, 0)

    def sums(u, c):
        comps = []
        for ff in range(2):
            f = 2 * u + ff
            a, b = lh[f, 0], lh[f, 1]
            m = dot(jnp.concatenate([a, b, a], axis=1), jnp.concatenate([xh[f, 0], xh[f, 0], xh[f, 1]], axis=0))
            comps += [m[:96], m[96:]]
        at = pl.ds(pl.multiple_of(8 * u, 8), 8)
        for h in range(2):
            t = turn32([v[:, h * 128 : h * 128 + 128] for v in comps])
            for zz in range(4):
                for i in range(4):
                    xx = (x + (0, 1, 3, 2)[i]) % 4
                    r = [72 + 8 * p if i == 3 else 24 * p + 8 * i for p in range(3)]
                    cf[zz, h, xx, 0, at, :] = t[zz][r[0] : r[0] + 8]
                    cf[zz, h, xx, 1, at, :] = t[zz][r[1] : r[1] + 8]
                    cmix[zz, h, xx, u] = t[zz][r[2] : r[2] + 8]
        return c

    place = (x, y, z)
    copies = []

    ORDER = (2, 1, 3, 0)

    def go(n, axis, r, src, dst):
        c = pltpu.make_async_remote_copy(
            src, dst, rs_send.at[n], rs_recv.at[n], device_id=along(axis, r), device_id_type=MESH
        )
        c.start()
        copies.append(c)
        return c

    def first_stage(share, axis, second, src, dst):
        groups = {}
        for k in ORDER:
            to = (place[second] + k) % 4
            groups[k] = [
                go(12 * share + 3 * k + r - 1, axis, r, src.at[(place[axis] + r) % 4, to], dst.at[r, to])
                for r in range(1, 4)
            ]
        return groups

    def landed(group):
        for c in group:
            c.wait_recv()

    def rows_a(zz, hh, xx, ll):
        return cf[zz, hh, xx, ll, 0:48, :]

    def pack_a(n, c):
        zz, hh, xx = n // 8, (n // 4) % 2, n % 4
        for ll in range(2):
            s1a[xx, 2 * hh + ll, zz] = rows_a(zz, hh, xx, ll).astype(BF16)
        return c

    l8 = lane((8, 128)) // 16

    def rows_bc(zz, hh, xx):
        mixes = [cmix[zz, hh, xx, u] for u in range(9)]
        tails = ([], [])
        for u in range(0, 8, 2):
            a, b = mixes[u], mixes[u + 1]
            tails[0].append(jnp.where(sub8 < 4, a, pltpu.roll(b, 4, 0)))
            tails[1].append(jnp.where(sub8 < 4, pltpu.roll(a, 4, 0), b))
        d = (xx - x + 4) % 4
        i = distance(d)
        m0, m1, mm = (mass[pl.ds(pl.multiple_of(row(i, p), 8), 8), :] for p in range(3))
        for ll, (m8, m4, last) in enumerate(
            ((m0, pltpu.roll(mm, 4, 0), mixes[8]), (m1, mm, pltpu.roll(mixes[8], 4, 0)))
        ):
            v = jnp.where(l8 < 2, pltpu.roll(m8, 4, 0), jnp.where(l8 < 4, m8, m4))
            vh = v.astype(BF16).astype(F32)
            v = jnp.where(l8 % 2 == 0, vh, v - vh)
            tails[ll].append(jnp.where(sub8 < 4, last, v))
        return [
            (
                jnp.concatenate([cf[zz, hh, xx, ll, 48:72, :], tails[ll][0]], axis=0),
                jnp.concatenate(tails[ll][1:], axis=0),
            )
            for ll in range(2)
        ]

    def pack_bc(n, c):
        zz, hh, xx = n // 8, (n // 4) % 2, n % 4
        for ll, (b, c_) in enumerate(rows_bc(zz, hh, xx)):
            s1b[2 * hh + ll, zz, xx] = b.astype(BF16)
            s1c[zz, xx, 2 * hh + ll] = c_.astype(BF16)
        return c

    lax.fori_loop(0, 6, sums, 0, unroll=6)
    lax.fori_loop(0, 32, pack_a, 0)
    g1a = first_stage(0, 0, 1, s1a, r1a)
    lax.fori_loop(6, 9, sums, 0, unroll=3)
    lax.fori_loop(0, 32, pack_bc, 0)
    g1b = first_stage(1, 1, 2, s1b, r1b)
    g1c = first_stage(2, 2, 0, s1c, r1c)

    def keep_a(n, c):
        for ll in range(2):
            own_a[2 * (n % 2) + ll, n // 2] = rows_a(n // 2, n % 2, x, ll)
        return c

    def keep_b(n, c):
        both = rows_bc(n // 4, yh, n % 4)
        own_b[n // 4, n % 4] = jnp.where(yl == 0, both[0][0], both[1][0])
        return c

    def keep_c(n, c):
        for ll, (_, v) in enumerate(rows_bc(z, n // 4, n % 4)):
            own_c[n % 4, 2 * (n // 4) + ll] = v
        return c

    lax.fori_loop(0, 8, keep_a, 0)
    lax.fori_loop(0, 16, keep_b, 0)
    lax.fori_loop(0, 8, keep_c, 0)

    shares = (
        (g1a, own_a, r1a, s2a, r2a, s3a, r3a, 1, 2),
        (g1b, own_b, r1b, s2b, r2b, s3b, r3b, 2, 0),
        (g1c, own_c, r1c, s2c, r2c, s3c, r3c, 0, 1),
    )
    g2 = ([], [], [])
    for k in ORDER:
        for share, (g1, own, r1, s2, r2, s3, r3, second, third) in enumerate(shares):
            landed(g1[k])
            to = (place[second] + k) % 4
            for j in range(4):
                total = own[to, j] + (r1[1, to, j].astype(F32) + r1[2, to, j].astype(F32)) + r1[3, to, j].astype(F32)
                if k:
                    s2[to, j] = total.astype(BF16)
                else:
                    own[to, j] = total
            if k:
                g2[share].append(go(36 + 3 * share + k - 1, second, k, s2.at[to], r2.at[k]))
    g3 = []
    for share, (g1, own, r1, s2, r2, s3, r3, second, third) in enumerate(shares):
        landed(g2[share])
        for j in range(4):
            s3[j] = own[place[second], j] + (r2[1, j].astype(F32) + r2[2, j].astype(F32)) + r2[3, j].astype(F32)
        g3.append(
            [
                go(45 + 3 * share + k - 1, third, k, s3.at[(place[third] + k) % 4], r3.at[k])
                for k in range(1, 4)
            ]
        )

    def add_third(held, got, axis):
        return held[place[axis]] + (got[1] + got[2]) + got[3]

    g3a, g3b, g3c = g3
    landed(g3a)
    part_a = add_third(s3a, r3a, 2)
    landed(g3b)
    part_b = add_third(s3b, r3b, 0)
    landed(g3c)
    part_c = add_third(s3c, r3c, 1)

    v = jnp.concatenate([part_a, part_b, part_c], axis=0)
    pairs = []
    for u in range(9):
        tail = v[72 + 8 * (u // 2) : 80 + 8 * (u // 2)]
        if u % 2:
            tail = pltpu.roll(tail, 4, 0)
        both = jnp.concatenate([v[8 * u : 8 * u + 8], tail], axis=0)
        comps = [both] + [pltpu.roll(both, 128 - 32 * i, 1) for i in range(1, 4)]
        pairs += [(comps[0], comps[1]), (comps[2], comps[3])]
    s = [w * (1.0 / 36.0) for w in inverse36(pairs)]
    block = lane((16, 128)) // 32
    cols = []
    for b in range(0, 36, 4):
        w = s[b]
        for i in range(1, 4):
            w = jnp.where(block == i, pltpu.roll(s[b + i], 32 * i, 1), w)
        cols.append(w)
    high, low = split(jnp.concatenate(cols, axis=1))
    o = dot(jnp.concatenate([high, low], axis=0), perm[...], NT)
    out[...] = (o[:16] + o[16:])[:12]
    m = v[104:112]
    m = m + pltpu.roll(m, 112, 1)
    l128 = lane((8, 128))
    for k in range(12):
        out_mass[k] = jnp.sum(jnp.where((sub8 == 4 + k % 4) & (l128 == 32 * (k // 4)), m, 0.0))
    for c in copies:
        c.wait_send()
    for c in started:
        c.wait_send()


def per_device(images, references, class_prior):
    hbm = pl.BlockSpec(memory_space=pl.ANY)
    smem = pl.BlockSpec(memory_space=pltpu.SMEM)
    rows = (48, 32, 32)
    return pl.pallas_call(
        kernel,
        out_shape=(jax.ShapeDtypeStruct((12, BAND), F32), jax.ShapeDtypeStruct((12,), F32)),
        in_specs=[hbm, hbm, hbm],
        out_specs=(pl.BlockSpec(memory_space=pltpu.VMEM), smem),
        scratch_shapes=[
            pltpu.SMEM((12,), F32),
            pltpu.VMEM((64, 9216), BF16),
            pltpu.VMEM((BAND, BAND), BF16),
            pltpu.VMEM((12, 16, 9216), BF16),
            pltpu.VMEM((128, BAND), BF16),
            pltpu.VMEM((2, 36, 64, 256), BF16),
            pltpu.VMEM((HALF, 2, 256, 256), BF16),
            pltpu.VMEM((8, 864, 128), BF16),
            pltpu.VMEM((HALF, 2, 96, 256), F32),
            pltpu.VMEM((4, 2, HALF, 2, 8, 128), F32),
            pltpu.VMEM((8, 16, 128), F32),
            pltpu.VMEM((36, 96, 128), F32),
            pltpu.VMEM((2, 2, 8, 128), F32),
            pltpu.VMEM((HALF, 2, 192, 256), BF16),
            pltpu.VMEM((96, 128), F32),
            pltpu.VMEM((4, 2, 4, 2, 72, 128), F32),
            pltpu.VMEM((4, 2, 4, 9, 8, 128), F32),
            *[pltpu.VMEM((4, 4, r, 128), F32) for r in rows],
            *[pltpu.VMEM((4, 4, 4, r, 128), BF16) for r in rows],
            *[pltpu.VMEM((4, 4, 4, r, 128), BF16) for r in rows],
            *[pltpu.VMEM((4, 4, r, 128), BF16) for r in rows],
            *[pltpu.VMEM((4, 4, r, 128), BF16) for r in rows],
            *[pltpu.VMEM((4, r, 128), F32) for r in rows],
            *[pltpu.VMEM((4, r, 128), F32) for r in rows],
            pltpu.SemaphoreType.DMA((14,)),
            pltpu.SemaphoreType.DMA((28,)),
            pltpu.SemaphoreType.DMA((28,)),
            pltpu.SemaphoreType.DMA((8,)),
            pltpu.SemaphoreType.DMA((8,)),
            pltpu.SemaphoreType.DMA((2,)),
            pltpu.SemaphoreType.DMA((2,)),
            pltpu.SemaphoreType.DMA((54,)),
            pltpu.SemaphoreType.DMA((54,)),
        ],
        compiler_params=pltpu.CompilerParams(
            collective_id=0, has_side_effects=True, vmem_limit_bytes=56 * 1024 * 1024
        ),
        name="em_pass",
    )(class_prior, images, references)


def solution(mesh):
    placed = (P(("img", "ref"), None), P("ref", None), P("ref"))
    return jax.shard_map(
        per_device,
        mesh=mesh,
        in_specs=placed,
        out_specs=(P("ref", "img"), P("ref")),
        check_vma=False,
    )
```

```python
import math
import jax
import jax.numpy as jnp
from jax import lax
from jax.experimental import pallas as pl
from jax.experimental.pallas import tpu as pltpu
from jax.sharding import PartitionSpec as P

ANG = 144
ROT = 36
TURN = 4
BAND = 1152
HALF = ROT // 2
F32 = jnp.float32
BF16 = jnp.bfloat16
MESH = pl.DeviceIdType.MESH

COS9 = [math.cos(2 * math.pi * m / 9) for m in range(9)]
SIN9 = [math.sin(2 * math.pi * m / 9) for m in range(9)]
ROOT3H = math.sqrt(3.0) / 2


def cos_sums(y0, e):
    t = e[0] + e[1] + e[3]
    top = y0 + e[2]
    base = y0 - 0.5 * e[2]
    out = [top + t]
    for f in (1, 2, 4):
        out.append(base + COS9[f % 9] * e[0] + COS9[2 * f % 9] * e[1] + COS9[4 * f % 9] * e[3])
    out.insert(3, top - 0.5 * t)
    return out


def sin_sums(o):
    h = ROOT3H * o[2]
    one = SIN9[1] * o[0] + SIN9[2] * o[1] + h + SIN9[4] * o[3]
    two = SIN9[2] * o[0] + SIN9[4] * o[1] - h - SIN9[1] * o[3]
    three = ROOT3H * (o[0] - o[1] + o[3])
    four = SIN9[4] * o[0] - SIN9[1] * o[1] + h - SIN9[2] * o[3]
    return [one, two, three, four]


def real9(y):
    e = [y[m] + y[9 - m] for m in range(1, 5)]
    o = [y[m] - y[9 - m] for m in range(1, 5)]
    s = sin_sums(o)
    return cos_sums(y[0], e), [None] + [-v for v in s]


def forward36(x):
    y0, y2, y1r, y1i = [], [], [], []
    for b2 in range(9):
        x0, x1, x2, x3 = (x[(9 * b1 + 4 * b2) % 36] for b1 in range(4))
        u0, u1, v0, v1 = x0 + x2, x0 - x2, x1 + x3, x3 - x1
        y0.append(u0 + v0)
        y2.append(u0 - v0)
        y1r.append(u1)
        y1i.append(v1)
    z0r, z0i = real9(y0)
    z2r, z2i = real9(y2)
    ur, ui = real9(y1r)
    vr, vi = real9(y1i)
    z1r, z1i = [None] * 9, [None] * 9
    z1r[0], z1i[0] = ur[0], vr[0]
    for f in range(1, 5):
        z1r[f], z1i[f] = ur[f] - vi[f], ui[f] + vr[f]
        z1r[9 - f], z1i[9 - f] = ur[f] + vi[f], vr[f] - ui[f]

    def at(f):
        f1, f2 = f % 4, f % 9
        if f1 in (0, 2):
            r, i = (z0r, z0i) if f1 == 0 else (z2r, z2i)
            if f2 == 0:
                return r[0], None
            return (r[f2], i[f2]) if f2 <= 4 else (r[9 - f2], -i[9 - f2])
        if f1 == 1:
            return z1r[f2], z1i[f2]
        g = (9 - f2) % 9
        return z1r[g], -z1i[g]

    return [(at(0)[0], at(18)[0])] + [at(f) for f in range(1, HALF)]


def inverse36(pairs):
    def spec(f):
        f %= 36
        if f == 0:
            return pairs[0][0], None
        if f == 18:
            return pairs[0][1], None
        if f < 18:
            return pairs[f]
        r, i = pairs[36 - f]
        return r, -i

    def find(f1, f2):
        return spec(next(f for f in range(36) if f % 4 == f1 and f % 9 == f2))

    def hermitian(f1):
        r0 = find(f1, 0)[0]
        z = [find(f1, f) for f in range(1, 5)]
        c = cos_sums(r0, [2.0 * r for r, _ in z])
        s = sin_sums([2.0 * i for _, i in z])
        y = [None] * 9
        y[0] = c[0]
        for m in range(1, 5):
            y[m], y[9 - m] = c[m] - s[m - 1], c[m] + s[m - 1]
        return y

    y0, y2 = hermitian(0), hermitian(2)
    z = [find(1, f) for f in range(9)]
    er = [z[f][0] + z[9 - f][0] for f in range(1, 5)]
    ei = [z[f][1] + z[9 - f][1] for f in range(1, 5)]
    dr = [z[f][0] - z[9 - f][0] for f in range(1, 5)]
    di = [z[f][1] - z[9 - f][1] for f in range(1, 5)]
    cr, ci = cos_sums(z[0][0], er), cos_sums(z[0][1], ei)
    sr, si = sin_sums(dr), sin_sums(di)
    y1r, y1i = [cr[0]] + [None] * 8, [ci[0]] + [None] * 8
    for m in range(1, 5):
        y1r[m], y1r[9 - m] = cr[m] - si[m - 1], cr[m] + si[m - 1]
        y1i[m], y1i[9 - m] = ci[m] + sr[m - 1], ci[m] - sr[m - 1]
    x = [None] * 36
    for b2 in range(9):
        p, q = y0[b2] + y2[b2], y0[b2] - y2[b2]
        a, b = 2.0 * y1r[b2], 2.0 * y1i[b2]
        for b1, v in enumerate((p + a, q - b, p - a, q + b)):
            x[(9 * b1 + 4 * b2) % 36] = v
    return x


def lane(shape):
    return lax.broadcasted_iota(jnp.int32, shape, len(shape) - 1)


def turn32(a):
    l = lane(a[0].shape)
    low = l < 64
    even = (l // 32) % 2 == 0
    b0 = jnp.where(low, a[0], pltpu.roll(a[2], 64, 1))
    b2 = jnp.where(low, pltpu.roll(a[0], 64, 1), a[2])
    b1 = jnp.where(low, a[1], pltpu.roll(a[3], 64, 1))
    b3 = jnp.where(low, pltpu.roll(a[1], 64, 1), a[3])
    out = []
    for p, q in ((b0, b1), (b2, b3)):
        out.append(jnp.where(even, p, pltpu.roll(q, 32, 1)))
        out.append(jnp.where(even, pltpu.roll(p, 96, 1), q))
    return out


def split(v):
    h = v.astype(BF16)
    return h, (v - h.astype(F32)).astype(BF16)


NT = (((1,), (1,)), ((), ()))
NN = (((1,), (0,)), ((), ()))


def dot(a, b, dims=NN):
    return lax.dot_general(a, b, dims, preferred_element_type=F32)


def kernel(
    prior_hbm, images_hbm, refs, out, out_mass,
    prior, images, perm, rows16, tload, x5, xh, tbuf, tf, tmix, offs, sh, stat, lh, mass, cf, cmix,
    own_a, own_b, own_c, s1a, s1b, s1c, r1a, r1b, r1c, s2a, s2b, s2c, r2a, r2b, r2c, s3a, s3b, s3c, r3a, r3b, r3c,
    load_sem, send_sem, recv_sem, off_send, off_recv, pair_send, pair_recv, rs_send, rs_recv,
):
    img, ref = lax.axis_index("img"), lax.axis_index("ref")
    z, yh = img // 2, img % 2
    x, yl, core = ref // 4, (ref // 2) % 2, ref % 2

    def dev(x_, y_, z_, c_):
        return {"img": z_ * 2 + y_ // 2, "ref": x_ * 4 + (y_ % 2) * 2 + c_}

    y = yh * 2 + yl
    xp, xm = (x + 1) % 4, (x + 3) % 4
    x2 = (x + 2) % 4
    to_xp, to_xm = dev(xp, y, z, core), dev(xm, y, z, core)
    to_yp, to_ym = dev(x, (y + 1) % 4, z, core), dev(x, (y + 3) % 4, z, core)
    sibling = dev(x, y, z, 1 - core)

    loads = []
    for k in range(12):
        c = pltpu.make_async_copy(refs.at[pl.ds(36 * k // 16 * 16, 16)], rows16.at[k], load_sem.at[k])
        c.start()
        loads.append(c)
    load_prior = pltpu.make_async_copy(prior_hbm, prior, load_sem.at[12])
    load_prior.start()
    load_images = pltpu.make_async_copy(images_hbm, images, load_sem.at[13])
    load_images.start()

    def along(axis, r):
        x_, y_, z_ = ((v + r * (a == axis)) % 4 for a, v in enumerate((x, y, z)))
        return dev(x_, y_, z_, core)

    def away(d):
        return dev((x + d // 2) % 4, yh * 2 + (yl + d) % 2, z, core)

    barrier = pltpu.get_barrier_semaphore()
    partners = [along(a, r) for a in range(3) for r in range(1, 4)] + [away(d) for d in (3, 5, 7)] + [sibling]
    for p in partners:
        pl.semaphore_signal(barrier, inc=1, device_id=p, device_id_type=MESH)
    def permutation(n, c):
        i = n * 128 + lax.broadcasted_iota(jnp.int32, (128, 128), 0)
        cycle = jnp.zeros_like(i)
        for q in range(1, 8):
            cycle = cycle + jnp.where(i >= ANG * q, 1, 0)
        i = i - ANG * cycle
        to = (i >> 2) * 32 + cycle * 4 + (i & 3) - lane((128, 128))
        for v in range(9):
            perm[pl.ds(pl.multiple_of(n * 128, 128), 128), v * 128 : v * 128 + 128] = jnp.where(
                to == 128 * v, 1.0, 0.0
            ).astype(BF16)
        return c

    lax.fori_loop(0, 9, permutation, 0)

    for c in loads:
        c.wait()
    norm = jnp.zeros((16, 128), F32)
    for g in range(8):
        tiles = []
        for k in range(12):
            at = 36 * k % 16
            tiles.append(rows16[k, :, g * BAND : (g + 1) * BAND].astype(F32)[at : at + 1])
        tiles.append(jnp.zeros((4, BAND), F32))
        t = jnp.concatenate(tiles, axis=0)
        for v in range(9):
            part = t[:, v * 128 : (v + 1) * 128]
            norm = norm + part * part
        tload[g * 16 : (g + 1) * 16, :] = t.astype(BF16)
    half_norm = 0.5 * jnp.sum(norm, axis=1, keepdims=True)
    rowid = lax.broadcasted_iota(jnp.int32, (16, 128), 0)
    load_prior.wait()
    pri = jnp.ones((16, 128), F32)
    for k in range(12):
        pri = jnp.where(rowid == k, prior[k], pri)
    slot = x * 2 + yl
    offs[slot] = jnp.log(pri) - half_norm

    sub8 = lax.broadcasted_iota(jnp.int32, (8, 128), 0)

    def arrange(v, c):
        o = dot(tload[...], perm[:, pl.ds(pl.multiple_of(v * 128, 128), 128)])
        halves = [turn32([o[(2 * zz + h) * 16 : (2 * zz + h) * 16 + 16] for zz in range(4)]) for h in range(2)]
        rows = []
        for i in range(4):
            a, b = halves[0][i], halves[1][i]
            rows += [a[:8], b[:8], jnp.where(sub8 < 4, a[8:], pltpu.roll(b[8:], 4, 0))]
        tbuf[slot, pl.ds(pl.multiple_of(96 * v, 32), 96), :] = jnp.concatenate(rows, axis=0).astype(BF16)
        return c

    lax.fori_loop(0, 9, arrange, 0, unroll=9)

    pl.semaphore_wait(barrier, len(partners))

    PIECES = ((0, 224), (224, 208), (432, 224), (656, 208))

    def piece(s, p):
        return tbuf.at[s, pl.ds(*PIECES[p])]

    started = []

    def send(s, p, target, n):
        c = pltpu.make_async_remote_copy(
            piece(s, p), piece(s, p), send_sem.at[n], recv_sem.at[n], device_id=target, device_id_type=MESH
        )
        c.start()
        started.append(c)

    def arrived(s, p, n):
        pltpu.make_async_copy(piece(s, p), piece(s, p), recv_sem.at[n]).wait()

    for k in range(2):
        send(slot, k, to_xp, k)
        send(slot, 2 + k, to_xm, 6 + k)
        send(slot, k, to_yp, 12 + k)
        send(slot, 2 + k, to_ym, 14 + k)
    for k in range(2):
        send(slot, 2 + k, to_xp, 2 + k)
        send(slot, k, to_xm, 4 + k)
    off_copies = []
    for d in range(1, 8):
        c = pltpu.make_async_remote_copy(
            offs.at[slot], offs.at[slot], off_send.at[d], off_recv.at[d], device_id=away(d), device_id_type=MESH
        )
        c.start()
        off_copies.append(c)
    s_m, s_p, s_2 = xm * 2 + yl, xp * 2 + yl, x2 * 2 + yl
    o_0, o_m, o_p, o_2 = x * 2 + 1 - yl, xm * 2 + 1 - yl, xp * 2 + 1 - yl, x2 * 2 + 1 - yl

    load_images.wait()
    for g in range(3):
        cols = slice(g * 384, g * 384 + 384)
        stacked = jnp.concatenate([images[:, q * BAND : (q + 1) * BAND] for q in range(8)], axis=0)
        o = dot(stacked, perm[:, cols])
        parts = [o[q * 64 : q * 64 + 64] for q in range(8)]
        for vv in range(3):
            v = 3 * g + vv
            for h in range(2):
                t = turn32([parts[2 * zz + h][:, vv * 128 : vv * 128 + 128] for zz in range(4)])
                for i in range(4):
                    x5[core, 4 * v + i, :, h * 128 : h * 128 + 128] = t[i].astype(BF16)
    swap = pltpu.make_async_remote_copy(
        x5.at[core], x5.at[core], pair_send.at[0], pair_recv.at[0], device_id=sibling, device_id_type=MESH
    )
    swap.start()

    for k in range(2):
        arrived(s_m, k, k)
        send(s_m, k, to_xp, 8 + k)
        send(s_m, k, to_yp, 16 + k)
        arrived(s_p, 2 + k, 6 + k)
        send(s_p, 2 + k, to_xm, 10 + k)
        send(s_p, 2 + k, to_ym, 22 + k)

    def image_spectra(c):
        def step(n, carry):
            t, h = n // 2, n % 2
            r0 = pl.multiple_of(t * 16, 16)
            lanes = pl.ds(pl.multiple_of(h * 128, 128), 128)
            p = forward36([x5[c, b, pl.ds(r0, 16), lanes].astype(F32) for b in range(36)])
            for f in range(HALF):
                for ri in range(2):
                    a, b = split(p[f][ri])
                    at = pl.ds(pl.multiple_of(ri * 128 + c * 64 + r0, 16), 16)
                    xh[f, 0, at, lanes] = a
                    xh[f, 1, at, lanes] = b
            return carry

        lax.fori_loop(0, 8, step, 0)

    image_spectra(core)
    for k in range(2):
        arrived(s_p, k, 4 + k)
        send(s_p, k, to_yp, 20 + k)
        arrived(s_m, 2 + k, 2 + k)
        send(s_m, 2 + k, to_ym, 18 + k)
    swap.wait()
    image_spectra(1 - core)
    for k in range(2):
        arrived(s_2, k, 8 + k)
        send(s_2, k, to_yp, 24 + k)
        arrived(s_2, 2 + k, 10 + k)
        send(s_2, 2 + k, to_ym, 26 + k)

    def distance(i):
        return jnp.where(i == 3, 2, jnp.where(i == 2, 3, i))

    def row(i, part):
        return jnp.where(i == 3, 72 + 8 * part, 24 * part + 8 * i)

    def template_spectra(i, ll):
        s = (x + distance(i)) % 4 * 2 + ll
        raw = []
        for b in range(HALF):
            two = tbuf[s, 48 * b : 48 * b + 48, :].astype(F32)
            raw += [two[:24], two[24:]]
        p = forward36(raw)
        at = pl.ds(pl.multiple_of(row(i, ll), 8), 8)
        for f in range(HALF):
            for ri in range(2):
                v = p[f][ri]
                tf[f, ri, at, 0:128] = v[0:8]
                tf[f, ri, at, 128:256] = v[8:16]
                tmix[i, ll, f, ri] = v[16:24]

    def score_part(members, lo, hi):
        count = hi - lo

        def score(f, c):
            for ri in range(2):
                for i in members:
                    a, b = tmix[i, 0, f, ri], tmix[i, 1, f, ri]
                    at = 88 if i == 3 else 48 + 8 * i
                    tf[f, ri, at : at + 8, 0:128] = jnp.where(sub8 < 4, a, pltpu.roll(b, 4, 0))
                    tf[f, ri, at : at + 8, 128:256] = jnp.where(sub8 < 4, pltpu.roll(a, 4, 0), b)
            high, low = split(jnp.concatenate([tf[f, 0, lo:hi, :], tf[f, 1, lo:hi, :]], axis=0))
            m = dot(jnp.concatenate([high, low], axis=0), xh[f, 0], NT)
            m = m[: 2 * count] + (m[2 * count :] + dot(high, xh[f, 1], NT))
            rr, ri_, ir, ii = m[:count, :128], m[:count, 128:], m[count:, :128], m[count:, 128:]
            first = f == 0
            sh[2 * f, lo:hi, :] = jnp.where(first, rr, rr + ii)
            sh[2 * f + 1, lo:hi, :] = jnp.where(first, ii, ri_ - ir)
            return c

        lax.fori_loop(0, HALF, score, 0, unroll=9)

    def own_row(i, c):
        template_spectra(i, yl)
        return c

    def other_row(i, c):
        template_spectra(i, 1 - yl)
        return c

    lax.fori_loop(0, 4, own_row, 0)
    for p in range(4):
        arrived(o_0, p, 12 + p)
    for p in range(4):
        arrived(o_m, p, 16 + p)
        arrived(o_p, p, 20 + p)
    lax.fori_loop(0, 3, other_row, 0)
    for p in range(4):
        arrived(o_2, p, 24 + p)
    lax.fori_loop(3, 4, other_row, 0)
    score_part((0, 1, 2, 3), 0, 96)
    for c in off_copies:
        c.wait()

    def to_turns(off, rows, top):
        p = [(sh[2 * f, rows, :], sh[2 * f + 1, rows, :]) for f in range(HALF)]
        s = inverse36(p)
        for r in range(36):
            v = s[r] * (1.0 / 36.0) + off
            sh[r, rows, :] = v
            top = jnp.maximum(top, v)
        return top

    def rows_of(n, c):
        i = jnp.where(n < 9, n % 3, 3)
        part = jnp.where(n < 9, n // 3, n - 9)
        at = (x + distance(i)) % 4 * 2
        a, b = offs[at], offs[at + 1]
        last = jnp.where(sub8 < 4, a[8:], pltpu.roll(b[8:], 4, 0))
        off = jnp.where(part == 0, a[:8], jnp.where(part == 1, b[:8], last))
        return to_turns(off, pl.ds(pl.multiple_of(n * 8, 8), 8), c)

    top8 = lax.fori_loop(0, 12, rows_of, jnp.full((8, 128), -jnp.inf, F32))
    top = jnp.max(top8, axis=0, keepdims=True)

    def raise_(n, c):
        rows = pl.ds(pl.multiple_of(n * 8, 8), 8)
        for r in range(36):
            e = jnp.exp(sh[r, rows, :] - top)
            sh[r, rows, :] = e
            c = c + e
        return c

    total = jnp.sum(lax.fori_loop(0, 12, raise_, jnp.zeros((8, 128), F32), unroll=2), axis=0, keepdims=True)
    stat[0, 0] = jnp.broadcast_to(top, (8, 128))
    stat[0, 1] = jnp.broadcast_to(total, (8, 128))
    share = pltpu.make_async_remote_copy(
        stat.at[0], stat.at[1], pair_send.at[1], pair_recv.at[1], device_id=sibling, device_id_type=MESH
    )
    share.start()
    share.wait()
    top_o, total_o = stat[1, 0][:1], stat[1, 1][:1]
    peak = jnp.maximum(top, top_o)
    mine = jnp.exp(top - peak)
    scale = mine / (total * mine + total_o * jnp.exp(top_o - peak))

    def weigh(n, c):
        rows = pl.ds(pl.multiple_of(n * 16, 16), 16)
        upper = pl.ds(pl.multiple_of(n * 16 + 96, 16), 16)
        w = [(sh[r, rows, :] * scale).astype(BF16).astype(F32) for r in range(36)]
        p = forward36(w)
        mass[rows, :] = jnp.broadcast_to(jnp.sum(p[0][0], axis=1, keepdims=True), (16, 128))
        none = jnp.zeros((16, 128), BF16)
        for f in range(HALF):
            for part, (r, i) in enumerate(zip(split(p[f][0]), split(p[f][1]))):
                lh[f, part, rows, 0:128] = r
                lh[f, part, rows, 128:256] = none if f == 0 else i
                lh[f, part, upper, 0:128] = none if f == 0 else -i
                lh[f, part, upper, 128:256] = i if f == 0 else r
        return c

    lax.fori_loop(0, 6, weigh, 0)

    def sums(u, c):
        comps = []
        for ff in range(2):
            f = 2 * u + ff
            a, b = lh[f, 0], lh[f, 1]
            m = dot(jnp.concatenate([a, b, a], axis=1), jnp.concatenate([xh[f, 0], xh[f, 0], xh[f, 1]], axis=0))
            comps += [m[:96], m[96:]]
        at = pl.ds(pl.multiple_of(8 * u, 8), 8)
        for h in range(2):
            t = turn32([v[:, h * 128 : h * 128 + 128] for v in comps])
            for zz in range(4):
                for i in range(4):
                    xx = (x + (0, 1, 3, 2)[i]) % 4
                    r = [72 + 8 * p if i == 3 else 24 * p + 8 * i for p in range(3)]
                    cf[zz, h, xx, 0, at, :] = t[zz][r[0] : r[0] + 8]
                    cf[zz, h, xx, 1, at, :] = t[zz][r[1] : r[1] + 8]
                    cmix[zz, h, xx, u] = t[zz][r[2] : r[2] + 8]
        return c

    place = (x, y, z)
    copies = []

    ORDER = (2, 1, 3, 0)

    def go(n, axis, r, src, dst):
        c = pltpu.make_async_remote_copy(
            src, dst, rs_send.at[n], rs_recv.at[n], device_id=along(axis, r), device_id_type=MESH
        )
        c.start()
        copies.append(c)
        return c

    def first_stage(share, axis, second, src, dst):
        groups = {}
        for k in ORDER:
            to = (place[second] + k) % 4
            groups[k] = [
                go(12 * share + 3 * k + r - 1, axis, r, src.at[(place[axis] + r) % 4, to], dst.at[r, to])
                for r in range(1, 4)
            ]
        return groups

    def landed(group):
        for c in group:
            c.wait_recv()

    def rows_a(zz, hh, xx, ll):
        return cf[zz, hh, xx, ll, 0:48, :]

    def pack_a(n, c):
        zz, hh, xx = n // 8, (n // 4) % 2, n % 4
        for ll in range(2):
            s1a[xx, 2 * hh + ll, zz] = rows_a(zz, hh, xx, ll).astype(BF16)
        return c

    l8 = lane((8, 128)) // 16

    def rows_bc(zz, hh, xx):
        mixes = [cmix[zz, hh, xx, u] for u in range(9)]
        tails = ([], [])
        for u in range(0, 8, 2):
            a, b = mixes[u], mixes[u + 1]
            tails[0].append(jnp.where(sub8 < 4, a, pltpu.roll(b, 4, 0)))
            tails[1].append(jnp.where(sub8 < 4, pltpu.roll(a, 4, 0), b))
        d = (xx - x + 4) % 4
        i = distance(d)
        m0, m1, mm = (mass[pl.ds(pl.multiple_of(row(i, p), 8), 8), :] for p in range(3))
        for ll, (m8, m4, last) in enumerate(
            ((m0, pltpu.roll(mm, 4, 0), mixes[8]), (m1, mm, pltpu.roll(mixes[8], 4, 0)))
        ):
            v = jnp.where(l8 < 2, pltpu.roll(m8, 4, 0), jnp.where(l8 < 4, m8, m4))
            vh = v.astype(BF16).astype(F32)
            v = jnp.where(l8 % 2 == 0, vh, v - vh)
            tails[ll].append(jnp.where(sub8 < 4, last, v))
        return [
            (
                jnp.concatenate([cf[zz, hh, xx, ll, 48:72, :], tails[ll][0]], axis=0),
                jnp.concatenate(tails[ll][1:], axis=0),
            )
            for ll in range(2)
        ]

    def pack_bc(n, c):
        zz, hh, xx = n // 8, (n // 4) % 2, n % 4
        for ll, (b, c_) in enumerate(rows_bc(zz, hh, xx)):
            s1b[2 * hh + ll, zz, xx] = b.astype(BF16)
            s1c[zz, xx, 2 * hh + ll] = c_.astype(BF16)
        return c

    lax.fori_loop(0, 6, sums, 0, unroll=6)
    lax.fori_loop(0, 32, pack_a, 0, unroll=4)
    g1a = first_stage(0, 0, 1, s1a, r1a)
    lax.fori_loop(6, 9, sums, 0, unroll=3)
    lax.fori_loop(0, 32, pack_bc, 0, unroll=4)
    g1b = first_stage(1, 1, 2, s1b, r1b)
    g1c = first_stage(2, 2, 0, s1c, r1c)

    def keep_a(n, c):
        for ll in range(2):
            own_a[2 * (n % 2) + ll, n // 2] = rows_a(n // 2, n % 2, x, ll)
        return c

    def keep_b(n, c):
        both = rows_bc(n // 4, yh, n % 4)
        own_b[n // 4, n % 4] = jnp.where(yl == 0, both[0][0], both[1][0])
        return c

    def keep_c(n, c):
        for ll, (_, v) in enumerate(rows_bc(z, n // 4, n % 4)):
            own_c[n % 4, 2 * (n // 4) + ll] = v
        return c

    lax.fori_loop(0, 8, keep_a, 0)
    lax.fori_loop(0, 16, keep_b, 0)
    lax.fori_loop(0, 8, keep_c, 0)

    shares = (
        (g1a, own_a, r1a, s2a, r2a, s3a, r3a, 1, 2),
        (g1b, own_b, r1b, s2b, r2b, s3b, r3b, 2, 0),
        (g1c, own_c, r1c, s2c, r2c, s3c, r3c, 0, 1),
    )
    g2 = ([], [], [])
    for k in ORDER:
        for share, (g1, own, r1, s2, r2, s3, r3, second, third) in enumerate(shares):
            landed(g1[k])
            to = (place[second] + k) % 4
            for j in range(4):
                total = own[to, j] + (r1[1, to, j].astype(F32) + r1[2, to, j].astype(F32)) + r1[3, to, j].astype(F32)
                if k:
                    s2[to, j] = total.astype(BF16)
                else:
                    own[to, j] = total
            if k:
                g2[share].append(go(36 + 3 * share + k - 1, second, k, s2.at[to], r2.at[k]))
    g3 = []
    for share, (g1, own, r1, s2, r2, s3, r3, second, third) in enumerate(shares):
        landed(g2[share])
        for j in range(4):
            s3[j] = own[place[second], j] + (r2[1, j].astype(F32) + r2[2, j].astype(F32)) + r2[3, j].astype(F32)
        g3.append(
            [
                go(45 + 3 * share + k - 1, third, k, s3.at[(place[third] + k) % 4], r3.at[k])
                for k in range(1, 4)
            ]
        )

    def add_third(held, got, axis):
        return held[place[axis]] + (got[1] + got[2]) + got[3]

    g3a, g3b, g3c = g3
    landed(g3a)
    part_a = add_third(s3a, r3a, 2)
    landed(g3b)
    part_b = add_third(s3b, r3b, 0)
    landed(g3c)
    part_c = add_third(s3c, r3c, 1)

    v = jnp.concatenate([part_a, part_b, part_c], axis=0)
    pairs = []
    for u in range(9):
        tail = v[72 + 8 * (u // 2) : 80 + 8 * (u // 2)]
        if u % 2:
            tail = pltpu.roll(tail, 4, 0)
        both = jnp.concatenate([v[8 * u : 8 * u + 8], tail], axis=0)
        comps = [both] + [pltpu.roll(both, 128 - 32 * i, 1) for i in range(1, 4)]
        pairs += [(comps[0], comps[1]), (comps[2], comps[3])]
    s = [w * (1.0 / 36.0) for w in inverse36(pairs)]
    block = lane((16, 128)) // 32
    cols = []
    for b in range(0, 36, 4):
        w = s[b]
        for i in range(1, 4):
            w = jnp.where(block == i, pltpu.roll(s[b + i], 32 * i, 1), w)
        cols.append(w)
    high, low = split(jnp.concatenate(cols, axis=1))
    o = dot(jnp.concatenate([high, low], axis=0), perm[...], NT)
    out[...] = (o[:16] + o[16:])[:12]
    m = v[104:112]
    m = m + pltpu.roll(m, 112, 1)
    l128 = lane((8, 128))
    for k in range(12):
        out_mass[k] = jnp.sum(jnp.where((sub8 == 4 + k % 4) & (l128 == 32 * (k // 4)), m, 0.0))
    for c in copies:
        c.wait_send()
    for c in started:
        c.wait_send()


def per_device(images, references, class_prior):
    hbm = pl.BlockSpec(memory_space=pl.ANY)
    smem = pl.BlockSpec(memory_space=pltpu.SMEM)
    rows = (48, 32, 32)
    return pl.pallas_call(
        kernel,
        out_shape=(jax.ShapeDtypeStruct((12, BAND), F32), jax.ShapeDtypeStruct((12,), F32)),
        in_specs=[hbm, hbm, hbm],
        out_specs=(pl.BlockSpec(memory_space=pltpu.VMEM), smem),
        scratch_shapes=[
            pltpu.SMEM((12,), F32),
            pltpu.VMEM((64, 9216), BF16),
            pltpu.VMEM((BAND, BAND), BF16),
            pltpu.VMEM((12, 16, 9216), BF16),
            pltpu.VMEM((128, BAND), BF16),
            pltpu.VMEM((2, 36, 64, 256), BF16),
            pltpu.VMEM((HALF, 2, 256, 256), BF16),
            pltpu.VMEM((8, 864, 128), BF16),
            pltpu.VMEM((HALF, 2, 96, 256), F32),
            pltpu.VMEM((4, 2, HALF, 2, 8, 128), F32),
            pltpu.VMEM((8, 16, 128), F32),
            pltpu.VMEM((36, 96, 128), F32),
            pltpu.VMEM((2, 2, 8, 128), F32),
            pltpu.VMEM((HALF, 2, 192, 256), BF16),
            pltpu.VMEM((96, 128), F32),
            pltpu.VMEM((4, 2, 4, 2, 72, 128), F32),
            pltpu.VMEM((4, 2, 4, 9, 8, 128), F32),
            *[pltpu.VMEM((4, 4, r, 128), F32) for r in rows],
            *[pltpu.VMEM((4, 4, 4, r, 128), BF16) for r in rows],
            *[pltpu.VMEM((4, 4, 4, r, 128), BF16) for r in rows],
            *[pltpu.VMEM((4, 4, r, 128), BF16) for r in rows],
            *[pltpu.VMEM((4, 4, r, 128), BF16) for r in rows],
            *[pltpu.VMEM((4, r, 128), F32) for r in rows],
            *[pltpu.VMEM((4, r, 128), F32) for r in rows],
            pltpu.SemaphoreType.DMA((14,)),
            pltpu.SemaphoreType.DMA((28,)),
            pltpu.SemaphoreType.DMA((28,)),
            pltpu.SemaphoreType.DMA((8,)),
            pltpu.SemaphoreType.DMA((8,)),
            pltpu.SemaphoreType.DMA((2,)),
            pltpu.SemaphoreType.DMA((2,)),
            pltpu.SemaphoreType.DMA((54,)),
            pltpu.SemaphoreType.DMA((54,)),
        ],
        compiler_params=pltpu.CompilerParams(
            collective_id=0, has_side_effects=True, vmem_limit_bytes=56 * 1024 * 1024
        ),
        name="em_pass",
    )(class_prior, images, references)


def solution(mesh):
    placed = (P(("img", "ref"), None), P("ref", None), P("ref"))
    return jax.shard_map(
        per_device,
        mesh=mesh,
        in_specs=placed,
        out_specs=(P("ref", "img"), P("ref")),
        check_vma=False,
    )
```
